512 devices in a mesh: row: 128 (over y, z_lo, x, core), col: 4 (over z_hi).
Axes of the slice: x: 4, y: 8, z: 8 (z_hi: 4, z_lo: 2; z = z_hi * 2 + z_lo), core: 2. Of those that a mesh axis runs over, the one named last changes fastest.
Arguments:
- tokens: bfloat16 [512, 128, 256], P('row', 'col'), may hold values from -6 to 6
- gain: float32 [256], replicated, may hold values from 0.25 to 1.75
- w_qkv: bfloat16 [256, 768], replicated, may hold values from -0.375 to 0.375
- head_scale: float32 [4], replicated, may hold values from 3 to 12
- w_out: bfloat16 [256, 256], replicated, may hold values from -0.375 to 0.375
- w_merge: bfloat16 [1024, 512], replicated, may hold values from -0.1875 to 0.1875
- d_merged: bfloat16 [256, 64, 512], P('row', 'col'), may hold values from -0.25 to 0.25
- d_skip: bfloat16 [512, 128, 256], P('row', 'col'), may hold values from -0.25 to 0.25
Outputs:
- skip_out: bfloat16 [512, 128, 256], P('row', 'col')
- merged: bfloat16 [256, 64, 512], P('row', 'col')
- grad_tokens: bfloat16 [512, 128, 256], P('row', 'col')
- grad_qkv: float32 [256, 768], P('row', 'col')
- grad_out: float32 [256, 256], P('row', 'col')
- grad_merge: float32 [1024, 512], P('row', 'col')
- grad_gain: float32 [256], replicated
- grad_scale: float32 [4], replicated
The draws below stay inside these ranges and needn't reach their ends.
All inputs are finite; a program needn't handle non-finite values.
Results may differ from the reference program's by a relative error of at most 0.012.
The reference program's roundings to bfloat16 on the way count: a program that leaves them out, or rounds other values in their place, can miss the bound.
Values may be sent and summed in bfloat16 or wider, within the bound.
A program may use at most 64 MiB of HBM per device.

```python
import math
import jax
import jax.numpy as jnp
import numpy as np
from jax import lax

D = 256
DM = 512
HEAD_DIM = 64
RADIUS = 3
TILE_R = 4
TILE_C = 16
HEADS = 4
H = 512
IMAGE_ROWS = 512
W = 128
N_ROW = 128
N_COL = 4


def block_scale(key, dims, cuts, least, top_value):
    def one(axis_at, blocks):
        steps = jax.random.uniform(jax.random.fold_in(jax.random.fold_in(key, 6), axis_at), (blocks,), jnp.float32, least / len(cuts), top_value / len(cuts))
        return jnp.repeat(jnp.exp(steps), dims[axis_at] // blocks).reshape((-1,) + (1,) * (len(dims) - axis_at - 1))

    factor_of = one(*cuts[0])
    for cut in cuts[1:]:
        factor_of = factor_of * one(*cut)
    return factor_of


def centred(rng, extent, scale, most, cuts=(), kind=jnp.bfloat16):
    values = scale * jax.random.normal(rng, extent, jnp.float32)
    if cuts:
        values = values * block_scale(rng, extent, cuts, -0.22, 0.18)
    return jnp.clip(values, -most, most).astype(kind)


def setup_inputs(seed: int = 0) -> dict:
    key_list = jax.random.split(jax.random.key(seed), 9)
    return {
        "tokens": centred(key_list[0], (H, W, D), 1.0, 6.0, ((0, 128), (1, 4))),
        "gain": jnp.clip(1.0 + 0.15 * jax.random.normal(key_list[1], (D,), jnp.float32), 0.25, 1.75),
        "w_qkv": centred(key_list[2], (D, 3 * D), D ** -0.5, 0.375),
        "head_scale": jnp.clip(jnp.exp(jax.random.uniform(key_list[3], (HEADS,), jnp.float32, math.log(3.0), math.log(12.0))), 3.0, 12.0),
        "w_out": centred(key_list[4], (D, D), D ** -0.5, 0.375),
        "w_merge": centred(key_list[5], (4 * D, DM), (4 * D) ** -0.5, 0.1875),
        "d_merged": centred(key_list[6], (H // 2, W // 2, DM), (N_ROW * N_COL) ** -0.5, 0.25, ((0, 128), (1, 4))),
        "d_skip": centred(key_list[7], (H, W, D), (N_ROW * N_COL) ** -0.5, 0.25, ((0, 128), (1, 4))),
    }


EPS = 1e-06

def rounded(value):
    return lax.optimization_barrier(value.astype(jnp.bfloat16))

def split_queries(block):
    rows, cols, feats = block.shape
    part = block.reshape(rows // TILE_R, TILE_R, cols // TILE_C, TILE_C, feats).transpose(0, 2, 1, 3, 4)
    return part.reshape(rows // TILE_R, cols // TILE_C, TILE_R * TILE_C, feats)

def join_queries(tiles, rows, cols):
    feats = tiles.shape[-1]
    part = tiles.reshape(rows // TILE_R, cols // TILE_C, TILE_R, TILE_C, feats).transpose(0, 2, 1, 3, 4)
    return part.reshape(rows, cols, feats)

def tile_tables(rows, cols):
    span_r = TILE_R + 2 * RADIUS
    span_c = TILE_C + 2 * RADIUS
    row_table = (np.arange(rows // TILE_R)[:, None] * TILE_R + np.arange(span_r)[None, :]).reshape(-1)
    col_table = (np.arange(cols // TILE_C)[:, None] * TILE_C + np.arange(span_c)[None, :]).reshape(-1)
    return (row_table, col_table)

def cut_tiles(padded, rows, cols):
    span_r = TILE_R + 2 * RADIUS
    span_c = TILE_C + 2 * RADIUS
    row_table, col_table = tile_tables(rows, cols)
    feats = padded.shape[-1]
    part = jnp.take(padded, jnp.asarray(row_table, jnp.int32), axis=0)
    part = jnp.take(part, jnp.asarray(col_table, jnp.int32), axis=1)
    part = part.reshape(rows // TILE_R, span_r, cols // TILE_C, span_c, feats).transpose(0, 2, 1, 3, 4)
    return part.reshape(rows // TILE_R, cols // TILE_C, span_r * span_c, feats)

def add_tiles(tiles, rows, cols):
    span_r = TILE_R + 2 * RADIUS
    span_c = TILE_C + 2 * RADIUS
    row_table, col_table = tile_tables(rows, cols)
    feats = tiles.shape[-1]
    part = tiles.reshape(rows // TILE_R, cols // TILE_C, span_r, span_c, feats).transpose(0, 2, 1, 3, 4)
    part = part.reshape(row_table.shape[0], col_table.shape[0], feats)
    total = jnp.zeros((rows + 2 * RADIUS, cols + 2 * RADIUS, feats), tiles.dtype)
    return total.at[jnp.asarray(row_table, jnp.int32)[:, None], jnp.asarray(col_table, jnp.int32)[None, :]].add(part)

def window_mask():
    span_c = TILE_C + 2 * RADIUS
    count = (TILE_R + 2 * RADIUS) * span_c
    query_r = np.arange(TILE_R * TILE_C) // TILE_C
    query_c = np.arange(TILE_R * TILE_C) % TILE_C
    key_r = np.arange(count) // span_c
    key_c = np.arange(count) % span_c
    diff_r = key_r[None, :] - query_r[:, None]
    diff_c = key_c[None, :] - query_c[:, None]
    return jnp.asarray((diff_r >= 0) & (diff_r <= 2 * RADIUS) & (diff_c >= 0) & (diff_c <= 2 * RADIUS))

def attend(q_tiles, kv_tiles, valid_tiles, heads):
    nrow, ncol, nq, width = q_tiles.shape
    nk = kv_tiles.shape[2]
    dim = width // heads
    query = q_tiles.astype(jnp.float32).reshape(nrow, ncol, nq, heads, dim)
    keys = kv_tiles[..., :width].astype(jnp.float32).reshape(nrow, ncol, nk, heads, dim)
    values = kv_tiles[..., width:].astype(jnp.float32).reshape(nrow, ncol, nk, heads, dim)
    scores = jnp.einsum('abqhe,abkhe->abhqk', query, keys)
    allowed = window_mask()[None, None, None] & valid_tiles[:, :, None, None, :]
    expo = jnp.where(allowed, jnp.exp(scores), 0.0)
    prob = expo / lax.optimization_barrier(jnp.sum(expo, axis=-1, keepdims=True))
    weights = rounded(prob).astype(jnp.float32)
    out = jnp.einsum('abhqk,abkhe->abqhe', weights, values)
    return (out.reshape(nrow, ncol, nq, width).astype(jnp.bfloat16), prob)

def attend_back(q_tiles, kv_tiles, prob, grad_tiles, heads):
    nrow, ncol, nq, width = q_tiles.shape
    nk = kv_tiles.shape[2]
    dim = width // heads
    query = q_tiles.astype(jnp.float32).reshape(nrow, ncol, nq, heads, dim)
    keys = kv_tiles[..., :width].astype(jnp.float32).reshape(nrow, ncol, nk, heads, dim)
    values = kv_tiles[..., width:].astype(jnp.float32).reshape(nrow, ncol, nk, heads, dim)
    grads = grad_tiles.astype(jnp.float32).reshape(nrow, ncol, nq, heads, dim)
    d_weights = jnp.einsum('abqhe,abkhe->abhqk', grads, values)
    d_scores = prob * (d_weights - lax.optimization_barrier(jnp.sum(d_weights * prob, axis=-1, keepdims=True)))
    score_grad = rounded(d_scores).astype(jnp.float32)
    weights = rounded(prob).astype(jnp.float32)
    d_query = jnp.einsum('abhqk,abkhe->abqhe', score_grad, keys)
    d_keys = jnp.einsum('abhqk,abqhe->abkhe', score_grad, query)
    d_values = jnp.einsum('abhqk,abqhe->abkhe', weights, grads)
    kv_grad = jnp.concatenate([d_keys.reshape(nrow, ncol, nk, width), d_values.reshape(nrow, ncol, nk, width)], axis=-1)
    return (d_query.reshape(nrow, ncol, nq, width), kv_grad)

def reference(tokens, gain, w_qkv, head_scale, w_out, w_merge, d_merged, d_skip):
    span_r = TILE_R + 2 * RADIUS
    x = tokens.astype(jnp.float32)
    inverse = lax.rsqrt(lax.optimization_barrier(jnp.mean(x * x, axis=-1, keepdims=True)) + EPS)
    normed = (x * inverse * gain).astype(jnp.bfloat16)
    flat_normed = normed.reshape(H * W, D)
    qkv = jnp.dot(flat_normed, w_qkv, preferred_element_type=jnp.float32).reshape(H, W, 3, HEADS, HEAD_DIM)
    query, key_raw, value = (qkv[:, :, 0], qkv[:, :, 1], qkv[:, :, 2])
    q_norm = lax.rsqrt(lax.optimization_barrier(jnp.sum(query * query, axis=-1, keepdims=True)) + EPS)
    k_norm = lax.rsqrt(lax.optimization_barrier(jnp.sum(key_raw * key_raw, axis=-1, keepdims=True)) + EPS)
    q_unit = query * q_norm
    k_unit = key_raw * k_norm
    q_hat = rounded((q_unit * head_scale[:, None]).reshape(H, W, D))
    kv = rounded(jnp.concatenate([k_unit.reshape(H, W, D), value.reshape(H, W, D)], axis=-1))
    kv_pad = jnp.pad(kv, ((RADIUS, RADIUS), (RADIUS, RADIUS), (0, 0)))
    grid_c = jnp.arange(W + 2 * RADIUS, dtype=jnp.int32) - RADIUS
    col_ok = (grid_c >= 0) & (grid_c < W)
    starts = jnp.arange(H // TILE_R, dtype=jnp.int32) * TILE_R

    def pieces(start):
        q_block = lax.dynamic_slice_in_dim(q_hat, start, TILE_R, 0)
        kv_block = lax.dynamic_slice_in_dim(kv_pad, start, span_r, 0)
        row_ids = start - RADIUS + jnp.arange(span_r, dtype=jnp.int32)
        first = start // IMAGE_ROWS * IMAGE_ROWS
        row_ok = (row_ids >= first) & (row_ids < first + IMAGE_ROWS)
        in_block = row_ok[:, None] & col_ok[None, :]
        q_tiles = split_queries(q_block)
        kv_tiles = cut_tiles(kv_block, TILE_R, W)
        valid_tiles = cut_tiles(in_block[:, :, None], TILE_R, W)[..., 0]
        return (q_tiles, kv_tiles, valid_tiles)

    def forward_rows(start):
        q_tiles, kv_tiles, valid_tiles = pieces(start)
        out, prob = attend(q_tiles, kv_tiles, valid_tiles, HEADS)
        return join_queries(out, TILE_R, W)
    attn = lax.map(forward_rows, starts).reshape(H, W, D)
    flat_attn = attn.reshape(H * W, D)
    proj = jnp.dot(flat_attn, w_out, preferred_element_type=jnp.float32).reshape(H, W, D)
    skip_out = (x + proj).astype(jnp.bfloat16)
    merge_in = skip_out.reshape(H // 2, 2, W // 2, 2, D).transpose(0, 2, 1, 3, 4).reshape(H // 2 * (W // 2), 4 * D)
    merged = jnp.dot(merge_in, w_merge, preferred_element_type=jnp.float32).astype(jnp.bfloat16).reshape(H // 2, W // 2, DM)
    flat_dm = d_merged.reshape(H // 2 * (W // 2), DM)
    grad_merge = jnp.dot(merge_in.T, flat_dm, preferred_element_type=jnp.float32)
    d_in = jnp.dot(flat_dm, w_merge.T, preferred_element_type=jnp.float32)
    d_in = d_in.reshape(H // 2, W // 2, 2, 2, D).transpose(0, 2, 1, 3, 4).reshape(H, W, D)
    d_y = d_skip.astype(jnp.float32) + d_in
    dy_b = d_y.astype(jnp.bfloat16).reshape(H * W, D)
    grad_out = jnp.dot(flat_attn.T, dy_b, preferred_element_type=jnp.float32)
    d_attn = jnp.dot(dy_b, w_out.T, preferred_element_type=jnp.float32).astype(jnp.bfloat16).reshape(H, W, D)

    def backward_rows(start):
        q_tiles, kv_tiles, valid_tiles = pieces(start)
        out, prob = attend(q_tiles, kv_tiles, valid_tiles, HEADS)
        g_block = lax.dynamic_slice_in_dim(d_attn, start, TILE_R, 0)
        d_q_tiles, d_kv_tiles = attend_back(q_tiles, kv_tiles, prob, split_queries(g_block), HEADS)
        d_kv_block = add_tiles(d_kv_tiles, TILE_R, W)[:, RADIUS:RADIUS + W]
        top = d_kv_block[:RADIUS]
        middle = d_kv_block[RADIUS:RADIUS + TILE_R]
        bottom = d_kv_block[RADIUS + TILE_R:]
        return (join_queries(d_q_tiles, TILE_R, W), top, middle, bottom)
    d_qrows, top, middle, bottom = lax.map(backward_rows, starts)
    d_qhat = d_qrows.reshape(H, W, D)
    top_next = jnp.concatenate([top[1:], jnp.zeros_like(top[:1])], axis=0)
    bottom_prev = jnp.concatenate([jnp.zeros_like(bottom[:1]), bottom[:-1]], axis=0)
    full = middle + jnp.pad(top_next, ((0, 0), (TILE_R - RADIUS, 0), (0, 0), (0, 0)))
    full = full + jnp.pad(bottom_prev, ((0, 0), (0, TILE_R - RADIUS), (0, 0), (0, 0)))
    d_kv = full.reshape(H, W, 2 * D)
    g_qhat = d_qhat.reshape(H, W, HEADS, HEAD_DIM)
    grad_scale = lax.optimization_barrier(jnp.sum(q_unit * g_qhat, axis=(0, 1, 3)))
    g_unit = g_qhat * head_scale[:, None]
    d_query = q_norm * (g_unit - q_unit * lax.optimization_barrier(jnp.sum(q_unit * g_unit, axis=-1, keepdims=True)))
    g_key = d_kv[:, :, :D].reshape(H, W, HEADS, HEAD_DIM)
    d_key = k_norm * (g_key - k_unit * lax.optimization_barrier(jnp.sum(k_unit * g_key, axis=-1, keepdims=True)))
    d_value = d_kv[:, :, D:].reshape(H, W, HEADS, HEAD_DIM)
    d_qkv = jnp.stack([d_query, d_key, d_value], axis=2).reshape(H * W, 3 * D).astype(jnp.bfloat16)
    grad_qkv = jnp.dot(flat_normed.T, d_qkv, preferred_element_type=jnp.float32)
    d_normed = jnp.dot(d_qkv, w_qkv.T, preferred_element_type=jnp.float32).reshape(H, W, D)
    grad_gain = lax.optimization_barrier(jnp.sum(x * inverse * d_normed, axis=(0, 1)))
    scaled = gain * d_normed
    g_x = inverse * scaled - x * inverse ** 3 * lax.optimization_barrier(jnp.mean(x * scaled, axis=-1, keepdims=True))
    grad_tokens = (d_y + g_x).astype(jnp.bfloat16)
    return (skip_out, merged, grad_tokens, grad_qkv, grad_out, grad_merge, grad_gain, grad_scale)
```

```python
import jax
import jax.numpy as jnp
import numpy as np
from jax import lax
from jax.experimental import pallas as pl
from jax.experimental.pallas import tpu as pltpu
from jax.sharding import PartitionSpec as P

RADIUS = 3
TILE_R = 4
TILE_C = 16
IMG_MAX = 512


EPS = 1e-06


MESH = pl.DeviceIdType.MESH
NX, NY, NZ = 4, 8, 8
F32, BF16 = jnp.float32, jnp.bfloat16


def place():
    row, col = lax.axis_index("row"), lax.axis_index("col")
    return row // 16, (row // 8) % 2, (row // 2) % 4, row % 2, col


def device(y, zl, x, core, col):
    return (((y * 2 + zl) * 4 + x) * 2 + core, col)


def peers():
    y, zl, x, core, col = place()
    z = col * 2 + zl
    out = {"core": (core, [(1 - core, device(y, zl, x, 1 - core, col))])}
    out["x"] = (x, [])
    for p in range(1, NX):
        t = (x + p) % NX
        out["x"][1].append((t, device(y, zl, t, core, col)))
    out["y"] = (y, [])
    for p in range(1, NY):
        t = (y + p) % NY
        out["y"][1].append((t, device(t, zl, x, core, col)))
    out["z"] = (z, [])
    for p in range(1, NZ):
        t = (z + p) % NZ
        out["z"][1].append((t, device(y, t % 2, x, core, t // 2)))
    return out


def start_copies(copies):
    for c in copies:
        c.start()
    return copies


def wait_copies(copies):
    for c in copies:
        c.wait()


def exchange(peer_list, source, slots, send, recv):
    return start_copies(
        [
            pltpu.make_async_remote_copy(
                src_ref=source(t),
                dst_ref=slots.at[p],
                send_sem=send.at[p],
                recv_sem=recv.at[p],
                device_id=dev,
                device_id_type=MESH,
            )
            for p, (t, dev) in enumerate(peer_list)
        ]
    )


def spread(mine, peer_list, slots, send, recv):
    return start_copies(
        [
            pltpu.make_async_remote_copy(
                src_ref=slots.at[mine],
                dst_ref=slots.at[mine],
                send_sem=send.at[p],
                recv_sem=recv.at[p],
                device_id=dev,
                device_id_type=MESH,
            )
            for p, (t, dev) in enumerate(peer_list)
        ]
    )


def rows_at(ref, index, size):
    return ref.at[:, pl.ds(pl.multiple_of(index * size, size), size), :]

def reduce_kernel(ga, gb, gs, perm, o_qkv, o_out, o_merge, o_gs,
                  sa1, ra1, sa2, ra2, sa3, ra3, sa4, ra4,
                  sb1, rb1, sb2, rb2, sb3, rb3, sb4, rb4,
                  g1, g2, g3, g4, tsem_a, tsem_b, tsem_g):
    near = peers()
    bar = pltpu.get_barrier_semaphore()
    for axis in ("core", "x", "y", "z"):
        for _, dev in near[axis][1]:
            pl.semaphore_signal(bar, inc=1, device_id=dev, device_id_type=MESH)
    core, x, y, z = (near[a][0] for a in ("core", "x", "y", "z"))
    sa1[...] = ga[:, pl.ds(pl.multiple_of((1 - core) * 128, 128), 128), :].astype(BF16)
    sb1[...] = gb[:, pl.ds(pl.multiple_of((1 - core) * 512, 512), 512), :].astype(BF16)
    g1[core] = gs[...]
    pl.semaphore_wait(bar, 1 + 3 + 7 + 7)

    def sems(table, stage):
        return table.at[0, pl.ds(7 * stage, 7)], table.at[1, pl.ds(7 * stage, 7)]

    ca = exchange(near["core"][1], lambda t: sa1, ra1, *sems(tsem_a, 0))
    cg = spread(core, near["core"][1], g1, *sems(tsem_g, 0))
    cb = exchange(near["core"][1], lambda t: sb1, rb1, *sems(tsem_b, 0))

    wait_copies(ca)
    sa2[...] = (ga[:, pl.ds(pl.multiple_of(core * 128, 128), 128), :] + ra1[0].astype(F32)).astype(BF16)
    ca = exchange(near["x"][1], lambda t: rows_at(sa2, t, 32), ra2, *sems(tsem_a, 1))
    wait_copies(cg)
    g2[x] = g1[0] + g1[1]
    cg = spread(x, near["x"][1], g2, *sems(tsem_g, 1))
    wait_copies(cb)
    sb2[...] = (gb[:, pl.ds(pl.multiple_of(core * 512, 512), 512), :] + rb1[0].astype(F32)).astype(BF16)
    cb = exchange(near["x"][1], lambda t: rows_at(sb2, t, 128), rb2, *sems(tsem_b, 1))

    wait_copies(ca)
    total = sa2[:, pl.ds(pl.multiple_of(x * 32, 32), 32), :].astype(F32)
    for p in range(3):
        total = total + ra2[p].astype(F32)
    sa3[...] = jnp.dot(perm[...], total.astype(BF16).reshape(128, 256), preferred_element_type=F32).astype(BF16).reshape(8, 16, 256)
    ca = exchange(near["y"][1], lambda t: sa3.at[t], ra3, *sems(tsem_a, 2))
    wait_copies(cg)
    g3[y] = (g2[0] + g2[1]) + (g2[2] + g2[3])
    cg = spread(y, near["y"][1], g3, *sems(tsem_g, 2))
    wait_copies(cb)
    total = sb2[:, pl.ds(pl.multiple_of(x * 128, 128), 128), :].astype(F32)
    for p in range(3):
        total = total + rb2[p].astype(F32)
    sb3[...] = total.astype(BF16)
    cb = exchange(near["y"][1], lambda t: rows_at(sb3, t, 16), rb3, *sems(tsem_b, 2))

    wait_copies(ca)
    total = sa3[y].astype(F32)
    for p in range(7):
        total = total + ra3[p].astype(F32)
    sa4[...] = total.reshape(2, 8, 256)
    ca = exchange(near["z"][1], lambda t: sa4.at[t // 4], ra4, *sems(tsem_a, 3))
    wait_copies(cg)
    g4[z] = ((g3[0] + g3[1]) + (g3[2] + g3[3])) + ((g3[4] + g3[5]) + (g3[6] + g3[7]))
    cg = spread(z, near["z"][1], g4, *sems(tsem_g, 3))
    wait_copies(cb)
    total = sb3[:, pl.ds(pl.multiple_of(y * 16, 16), 16), :].astype(F32)
    for p in range(7):
        total = total + rb3[p].astype(F32)
    sb4[...] = total
    cb = exchange(near["z"][1], lambda t: sb4.at[t // 2, pl.ds(pl.multiple_of(t % 2 * 8, 8), 8), :], rb4, *sems(tsem_b, 3))

    wait_copies(ca)
    total = sa4[z // 4]
    for p in range(7):
        total = total + ra4[p]
    part = z % 4
    piece = jnp.zeros((2, 256), F32)
    for k in range(4):
        piece = piece + jnp.where(part == k, total[2 * k : 2 * k + 2], 0.0)
    o_qkv[...] = piece[:, :192]
    o_out[...] = piece[:, 192:]
    wait_copies(cg)
    o_gs[...] = ((g4[0] + g4[1]) + (g4[2] + g4[3])) + ((g4[4] + g4[5]) + (g4[6] + g4[7]))
    wait_copies(cb)
    total = sb4[z // 2, pl.ds(pl.multiple_of(z % 2 * 8, 8), 8), :]
    for p in range(7):
        total = total + rb4[p]
    o_merge[...] = total


def slab_order():
    perm = np.zeros((128, 128), np.float32)
    for c in range(4):
        for yy in range(8):
            for k in range(4):
                perm[yy * 16 + c * 4 + k, c * 32 + yy * 4 + k] = 1
    return jnp.asarray(perm, BF16)


def reduce_all(grad_qkv, grad_out, grad_merge, gain, scale):
    a = jnp.concatenate([grad_qkv.reshape(256, 4, 192), grad_out.reshape(256, 4, 64)], axis=-1)
    a = a.reshape(8, 2, 4, 2, 2, 4, 256).transpose(5, 3, 2, 0, 1, 4, 6).reshape(4, 256, 256)
    b = grad_merge.reshape(8, 2, 4, 2, 8, 4, 128).transpose(5, 3, 2, 0, 1, 4, 6).reshape(4, 1024, 128)
    gs = jnp.concatenate([gain, scale, jnp.zeros(764, F32)]).reshape(8, 128)
    vmem = pl.BlockSpec(memory_space=pltpu.VMEM)
    V = pltpu.VMEM
    return pl.pallas_call(
        reduce_kernel,
        out_shape=(
            jax.ShapeDtypeStruct((2, 192), F32),
            jax.ShapeDtypeStruct((2, 64), F32),
            jax.ShapeDtypeStruct((8, 128), F32),
            jax.ShapeDtypeStruct((8, 128), F32),
        ),
        in_specs=[vmem] * 4,
        out_specs=(vmem,) * 4,
        scratch_shapes=[
            V((4, 128, 256), BF16), V((1, 4, 128, 256), BF16),
            V((4, 128, 256), BF16), V((3, 4, 32, 256), BF16),
            V((8, 16, 256), BF16), V((7, 16, 256), BF16),
            V((2, 8, 256), F32), V((7, 8, 256), F32),
            V((4, 512, 128), BF16), V((1, 4, 512, 128), BF16),
            V((4, 512, 128), BF16), V((3, 4, 128, 128), BF16),
            V((4, 128, 128), BF16), V((7, 4, 16, 128), BF16),
            V((4, 16, 128), F32), V((7, 8, 128), F32),
            V((2, 8, 128), F32), V((4, 8, 128), F32), V((8, 8, 128), F32), V((8, 8, 128), F32),
            pltpu.SemaphoreType.DMA((2, 28)), pltpu.SemaphoreType.DMA((2, 28)), pltpu.SemaphoreType.DMA((2, 28)),
        ],
        compiler_params=pltpu.CompilerParams(collective_id=0, has_side_effects=True, vmem_limit_bytes=48 * 2**20),
    )(a, b, gs, slab_order())


def extended(value, sides, width):
    for axis, dim in sides:
        count, length = (lax.axis_size(axis), value.shape[dim])
        up = [(i, (i + 1) % count) for i in range(count - 1)]
        down = [(j, i) for i, j in up]
        last = lax.slice_in_dim(value, length - width, length, axis=dim)
        initial = lax.slice_in_dim(value, 0, width, axis=dim)
        before = lax.ppermute(last, axis, up)
        after = lax.ppermute(initial, axis, down)
        value = jnp.concatenate([before, value, after], axis=dim)
    return value


def passed_along(value, axis, steps):
    count = lax.axis_size(axis)
    initial, last = (max(0, -steps), min(count, count - steps))
    return lax.ppermute(value, axis, [(source, source + steps) for source in range(initial, last)])


def split_queries(block):
    rows, cols, feats = block.shape
    part = block.reshape(rows // TILE_R, TILE_R, cols // TILE_C, TILE_C, feats).transpose(
        0, 2, 1, 3, 4
    )
    return part.reshape(rows // TILE_R, cols // TILE_C, TILE_R * TILE_C, feats)


def join_queries(tiles, rows, cols):
    feats = tiles.shape[-1]
    part = tiles.reshape(rows // TILE_R, cols // TILE_C, TILE_R, TILE_C, feats).transpose(
        0, 2, 1, 3, 4
    )
    return part.reshape(rows, cols, feats)


def cut_block(padded, cols):
    span_r = TILE_R + 2 * RADIUS
    span_c = TILE_C + 2 * RADIUS
    feats = padded.shape[-1]
    count = cols // TILE_C
    parts = [padded[:, j * TILE_C : j * TILE_C + span_c] for j in range(count)]
    return jnp.stack(parts, axis=0).reshape(1, count, span_r * span_c, feats)


def add_block(tiles, cols):
    span_r = TILE_R + 2 * RADIUS
    span_c = TILE_C + 2 * RADIUS
    feats = tiles.shape[-1]
    count = cols // TILE_C
    pieces = tiles.reshape(count, span_r, span_c, feats)
    total = jnp.zeros((span_r, cols + 2 * RADIUS, feats), tiles.dtype)
    for j in range(count):
        total = total.at[:, j * TILE_C : j * TILE_C + span_c].add(pieces[j])
    return total


def window_mask():
    span_c = TILE_C + 2 * RADIUS
    count = (TILE_R + 2 * RADIUS) * span_c
    query_r = np.arange(TILE_R * TILE_C) // TILE_C
    query_c = np.arange(TILE_R * TILE_C) % TILE_C
    key_r = np.arange(count) // span_c
    key_c = np.arange(count) % span_c
    diff_r = key_r[None, :] - query_r[:, None]
    diff_c = key_c[None, :] - query_c[:, None]
    return jnp.asarray(
        (diff_r >= 0) & (diff_r <= 2 * RADIUS) & (diff_c >= 0) & (diff_c <= 2 * RADIUS)
    )


def attend(q_tiles, kv_tiles, valid_tiles, heads):
    nrow, ncol, nq, width = q_tiles.shape
    nk = kv_tiles.shape[2]
    dim = width // heads
    query = q_tiles.reshape(nrow, ncol, nq, heads, dim)
    keys = kv_tiles[..., :width].reshape(nrow, ncol, nk, heads, dim)
    values = kv_tiles[..., width:].reshape(nrow, ncol, nk, heads, dim)
    scores = jnp.einsum("abqhe,abkhe->abhqk", query, keys, preferred_element_type=jnp.float32)
    allowed = window_mask()[None, None, None] & valid_tiles[:, :, None, None, :]
    expo = jnp.where(allowed, jnp.exp(scores), 0.0)
    prob = expo / jnp.sum(expo, axis=-1, keepdims=True)
    weights = prob.astype(jnp.bfloat16)
    out = jnp.einsum("abhqk,abkhe->abqhe", weights, values, preferred_element_type=jnp.float32)
    return (out.reshape(nrow, ncol, nq, width).astype(jnp.bfloat16), prob)


def attend_back(q_tiles, kv_tiles, prob, grad_tiles, heads):
    nrow, ncol, nq, width = q_tiles.shape
    nk = kv_tiles.shape[2]
    dim = width // heads
    query = q_tiles.reshape(nrow, ncol, nq, heads, dim)
    keys = kv_tiles[..., :width].reshape(nrow, ncol, nk, heads, dim)
    values = kv_tiles[..., width:].reshape(nrow, ncol, nk, heads, dim)
    grads = grad_tiles.reshape(nrow, ncol, nq, heads, dim)
    d_weights = jnp.einsum("abqhe,abkhe->abhqk", grads, values, preferred_element_type=jnp.float32)
    d_scores = prob * (d_weights - jnp.sum(d_weights * prob, axis=-1, keepdims=True))
    score_grad = d_scores.astype(jnp.bfloat16)
    weights = prob.astype(jnp.bfloat16)
    d_query = jnp.einsum("abhqk,abkhe->abqhe", score_grad, keys, preferred_element_type=jnp.float32)
    d_keys = jnp.einsum("abhqk,abqhe->abkhe", score_grad, query, preferred_element_type=jnp.float32)
    d_values = jnp.einsum("abhqk,abqhe->abkhe", weights, grads, preferred_element_type=jnp.float32)
    kv_grad = jnp.concatenate(
        [d_keys.reshape(nrow, ncol, nk, width), d_values.reshape(nrow, ncol, nk, width)], axis=-1
    )
    return (d_query.reshape(nrow, ncol, nq, width), kv_grad)


def on_device(tokens, gain, w_qkv, head_scale, w_out, w_merge, d_merged, d_skip):
    rows, cols, width = tokens.shape
    heads = head_scale.shape[0]
    head_dim = width // heads
    x = tokens.astype(jnp.float32)
    inverse = lax.rsqrt(jnp.mean(x * x, axis=-1, keepdims=True) + EPS)
    normed = (x * inverse * gain).astype(jnp.bfloat16)
    flat_normed = normed.reshape(rows * cols, width)
    qkv = jnp.dot(flat_normed, w_qkv, preferred_element_type=jnp.float32).reshape(
        rows, cols, 3, heads, head_dim
    )
    query, key_raw, value = (qkv[:, :, 0], qkv[:, :, 1], qkv[:, :, 2])
    q_norm = lax.rsqrt(jnp.sum(query * query, axis=-1, keepdims=True) + EPS)
    k_norm = lax.rsqrt(jnp.sum(key_raw * key_raw, axis=-1, keepdims=True) + EPS)
    q_unit = query * q_norm
    k_unit = key_raw * k_norm
    q_hat = (q_unit * head_scale[:, None]).reshape(rows, cols, width).astype(jnp.bfloat16)
    kv = jnp.concatenate(
        [k_unit.reshape(rows, cols, width), value.reshape(rows, cols, width)], axis=-1
    ).astype(jnp.bfloat16)
    kv_pad = extended(kv, (("row", 0), ("col", 1)), RADIUS)
    image_rows = min(IMG_MAX, rows * lax.axis_size("row"))
    row_start = lax.axis_index("row") * rows
    col_start = lax.axis_index("col") * cols
    first = row_start // image_rows * image_rows
    grid_r = jnp.arange(rows + 2 * RADIUS, dtype=jnp.int32) + row_start - RADIUS
    grid_c = jnp.arange(cols + 2 * RADIUS, dtype=jnp.int32) + col_start - RADIUS
    inside_r = (grid_r >= first) & (grid_r < first + image_rows)
    inside_c = (grid_c >= 0) & (grid_c < cols * lax.axis_size("col"))
    inside = inside_r[:, None] & inside_c[None, :]
    starts = jnp.arange(rows // TILE_R, dtype=jnp.int32) * TILE_R

    def pieces(start):
        q_tiles = split_queries(q_hat)
        kv_tiles = cut_block(kv_pad, cols)
        valid_tiles = cut_block(inside[:, :, None], cols)[..., 0]
        return (q_tiles, kv_tiles, valid_tiles)

    def forward_rows(start):
        q_tiles, kv_tiles, valid_tiles = pieces(start)
        out, prob = attend(q_tiles, kv_tiles, valid_tiles, heads)
        return join_queries(out, TILE_R, cols)

    attn = lax.map(forward_rows, starts).reshape(rows, cols, width)
    flat_attn = attn.reshape(rows * cols, width)
    proj = jnp.dot(flat_attn, w_out, preferred_element_type=jnp.float32).reshape(rows, cols, width)
    skip_out = (x + proj).astype(jnp.bfloat16)
    merge_in = skip_out.reshape(rows // 2, 2, cols // 2, 2, width).transpose(0, 2, 1, 3, 4)
    merge_in = merge_in.reshape(rows // 2 * (cols // 2), 4 * width)
    merged = jnp.dot(merge_in, w_merge, preferred_element_type=jnp.float32).astype(jnp.bfloat16)
    merged = merged.reshape(rows // 2, cols // 2, w_merge.shape[1])
    flat_dm = d_merged.reshape(rows // 2 * (cols // 2), d_merged.shape[-1])
    grad_merge = jnp.dot(merge_in.T, flat_dm, preferred_element_type=jnp.float32)
    d_in = jnp.dot(flat_dm, w_merge.T, preferred_element_type=jnp.float32)
    d_in = (
        d_in.reshape(rows // 2, cols // 2, 2, 2, width)
        .transpose(0, 2, 1, 3, 4)
        .reshape(rows, cols, width)
    )
    d_y = d_skip.astype(jnp.float32) + d_in
    dy_b = d_y.astype(jnp.bfloat16).reshape(rows * cols, width)
    grad_out = jnp.dot(flat_attn.T, dy_b, preferred_element_type=jnp.float32)
    d_attn = (
        jnp.dot(dy_b, w_out.T, preferred_element_type=jnp.float32)
        .astype(jnp.bfloat16)
        .reshape(rows, cols, width)
    )

    def backward_rows(start):
        q_tiles, kv_tiles, valid_tiles = pieces(start)
        out, prob = attend(q_tiles, kv_tiles, valid_tiles, heads)
        d_q_tiles, d_kv_tiles = attend_back(q_tiles, kv_tiles, prob, split_queries(d_attn), heads)
        d_kv_block = add_block(d_kv_tiles, cols)
        top = d_kv_block[:RADIUS]
        middle = d_kv_block[RADIUS : RADIUS + TILE_R]
        bottom = d_kv_block[RADIUS + TILE_R :]
        return (join_queries(d_q_tiles, TILE_R, cols), top, middle, bottom)

    d_qrows, top, middle, bottom = lax.map(backward_rows, starts)
    d_qhat = d_qrows.reshape(rows, cols, width)
    top_next = jnp.concatenate([top[1:], jnp.zeros_like(top)], axis=0)
    bottom_prev = jnp.concatenate([jnp.zeros_like(bottom), bottom[:-1]], axis=0)
    full = middle + jnp.pad(top_next, ((0, 0), (TILE_R - RADIUS, 0), (0, 0), (0, 0)))
    full = full + jnp.pad(bottom_prev, ((0, 0), (0, TILE_R - RADIUS), (0, 0), (0, 0)))
    full = full.reshape(rows, cols + 2 * RADIUS, 2 * width)
    d_kv_pad = jnp.concatenate([top[0], full, bottom[-1]], axis=0)
    left_rim = d_kv_pad[:, :RADIUS]
    right_rim = d_kv_pad[:, RADIUS + cols :]
    inner = d_kv_pad[:, RADIUS : RADIUS + cols]
    from_right = passed_along(left_rim.astype(jnp.bfloat16), "col", -1).astype(left_rim.dtype)
    from_left = passed_along(right_rim.astype(jnp.bfloat16), "col", 1).astype(right_rim.dtype)
    inner = inner.at[:, cols - RADIUS :].add(from_right)
    inner = inner.at[:, :RADIUS].add(from_left)
    top_rim = inner[:RADIUS]
    bottom_rim = inner[RADIUS + rows :]
    d_kv = inner[RADIUS : RADIUS + rows]
    from_below = passed_along(top_rim.astype(jnp.bfloat16), "row", -1).astype(top_rim.dtype)
    from_above = passed_along(bottom_rim.astype(jnp.bfloat16), "row", 1).astype(bottom_rim.dtype)
    d_kv = d_kv.at[rows - RADIUS :].add(from_below)
    d_kv = d_kv.at[:RADIUS].add(from_above)
    g_qhat = d_qhat.reshape(rows, cols, heads, head_dim)
    local_scale = jnp.sum(q_unit * g_qhat, axis=(0, 1, 3))
    g_unit = g_qhat * head_scale[:, None]
    d_query = q_norm * (g_unit - q_unit * jnp.sum(q_unit * g_unit, axis=-1, keepdims=True))
    g_key = d_kv[:, :, :width].reshape(rows, cols, heads, head_dim)
    d_key = k_norm * (g_key - k_unit * jnp.sum(k_unit * g_key, axis=-1, keepdims=True))
    d_value = d_kv[:, :, width:].reshape(rows, cols, heads, head_dim)
    d_qkv = (
        jnp.stack([d_query, d_key, d_value], axis=2)
        .reshape(rows * cols, 3 * width)
        .astype(jnp.bfloat16)
    )
    grad_qkv = jnp.dot(flat_normed.T, d_qkv, preferred_element_type=jnp.float32)
    d_normed = jnp.dot(d_qkv, w_qkv.T, preferred_element_type=jnp.float32).reshape(
        rows, cols, width
    )
    local_gain = jnp.sum(x * inverse * d_normed, axis=(0, 1))
    scaled = gain * d_normed
    g_x = inverse * scaled - x * inverse**3 * jnp.mean(x * scaled, axis=-1, keepdims=True)
    grad_tokens = (d_y + g_x).astype(jnp.bfloat16)
    o_qkv, o_out, o_merge, o_gs = reduce_all(grad_qkv, grad_out, grad_merge, local_gain, local_scale)
    flat = o_gs.reshape(-1)
    return (skip_out, merged, grad_tokens, o_qkv, o_out, o_merge, flat[:256], flat[256:260])


def solution(mesh):
    return jax.shard_map(
        on_device,
        mesh=mesh,
        in_specs=(
            P("row", "col", None),
            P(),
            P(),
            P(),
            P(),
            P(),
            P("row", "col", None),
            P("row", "col", None),
        ),
        out_specs=(
            P("row", "col", None),
            P("row", "col", None),
            P("row", "col", None),
            P("row", "col"),
            P("row", "col"),
            P("row", "col"),
            P(),
            P(),
        ),
        check_vma=False,
    )
```

```python
import jax
import jax.numpy as jnp
import numpy as np
from jax import lax
from jax.experimental import pallas as pl
from jax.experimental.pallas import tpu as pltpu
from jax.sharding import PartitionSpec as P

EPS = 1e-06
MESH = pl.DeviceIdType.MESH
NX, NY, NZ = 4, 8, 8
ROWS, COLS = 128, 4
F32, BF16 = jnp.float32, jnp.bfloat16
OWN, SIDE, SLOT, NK = 128, 96, 16, 416
HALO = NK - OWN


def place():
    row, col = lax.axis_index("row"), lax.axis_index("col")
    return row // 16, (row // 8) % 2, (row // 2) % 4, row % 2, col


def device(y, zl, x, core, col):
    return (((y * 2 + zl) * 4 + x) * 2 + core, col)


def peers():
    y, zl, x, core, col = place()
    z = col * 2 + zl
    out = {"core": (core, [(1 - core, device(y, zl, x, 1 - core, col))])}
    out["x"] = (x, [])
    for p in range(1, NX):
        t = (x + p) % NX
        out["x"][1].append((t, device(y, zl, t, core, col)))
    out["y"] = (y, [])
    for p in range(1, NY):
        t = (y + p) % NY
        out["y"][1].append((t, device(t, zl, x, core, col)))
    out["z"] = (z, [])
    for p in range(1, NZ):
        t = (z + p) % NZ
        out["z"][1].append((t, device(y, t % 2, x, core, t // 2)))
    return out


def start_copies(copies):
    for c in copies:
        c.start()
    return copies


def wait_copies(copies):
    for c in copies:
        c.wait()


def exchange(peer_list, source, slots, send, recv):
    return start_copies(
        [
            pltpu.make_async_remote_copy(
                src_ref=source(t),
                dst_ref=slots.at[p],
                send_sem=send.at[p],
                recv_sem=recv.at[p],
                device_id=dev,
                device_id_type=MESH,
            )
            for p, (t, dev) in enumerate(peer_list)
        ]
    )


def spread(mine, peer_list, slots, send, recv):
    return start_copies(
        [
            pltpu.make_async_remote_copy(
                src_ref=slots.at[mine],
                dst_ref=slots.at[mine],
                send_sem=send.at[p],
                recv_sem=recv.at[p],
                device_id=dev,
                device_id_type=MESH,
            )
            for p, (t, dev) in enumerate(peer_list)
        ]
    )


def rows_at(ref, index, size):
    return ref.at[:, pl.ds(pl.multiple_of(index * size, size), size), :]


def token_list():
    return [(2 * i + pr, 2 * j + pc) for pr in range(2) for pc in range(2) for i in range(2) for j in range(16)]


def slot_tokens(first_row, rows, first_col):
    return [(first_row + i // 3, first_col + i % 3) for i in range(3 * rows)]


def one_hot(rows, width, where):
    out = np.zeros((rows, width), np.float32)
    for i, j in where:
        out[i, j] = 1
    return out


def tables():
    own = token_list()
    order = one_hot(128, 128, [(p, r * 32 + c) for p, (r, c) in enumerate(own)])
    sent = [(0, 4, 29), (0, 4, 0), (1, 3, 29), (1, 3, 0), (0, 3, 29), (0, 3, 0)]
    pick = one_hot(
        96, 128,
        [(16 * s + i, r * 32 + c) for s, a in enumerate(sent) for i, (r, c) in enumerate(slot_tokens(*a))],
    )
    every = np.concatenate([np.eye(128)[32:], np.eye(128)[:96], pick])
    back = order @ every.T
    key_at = np.full((NK, 2), 1000)
    key_at[:128] = own
    key_at[128:224] = [(k // 32 - 3, k % 32) for k in range(96)]
    key_at[224:320] = [(k // 32 + 4, k % 32) for k in range(96)]
    held = [(0, 4, -3), (0, 4, 32), (-3, 3, -3), (-3, 3, 32), (4, 3, -3), (4, 3, 32)]
    for s, a in enumerate(held):
        got = slot_tokens(*a)
        key_at[320 + 16 * s : 320 + 16 * s + len(got)] = got
    gap = np.abs(key_at[:, None, :] - np.asarray(own)[None, :, :])
    near = (gap <= 3).all(axis=-1).astype(np.float32)
    row_a = one_hot(
        256, 256,
        [((((k * 4 + x) * 8 + y) * 2 + zl) * 2 + j, ((y * 2 + zl) * 4 + x) * 4 + k * 2 + j)
         for k in range(2) for x in range(4) for y in range(8) for zl in range(2) for j in range(2)],
    )
    row_b = one_hot(
        256, 256,
        [((((k * 4 + x) * 2 + t) * 2 + zl) * 8 + j, t * 128 + zl * 64 + x * 16 + k * 8 + j)
         for k in range(2) for x in range(4) for t in range(2) for zl in range(2) for j in range(8)],
    )
    ones = np.kron(np.eye(4), np.ones((64, 64)))
    slab = one_hot(
        128, 128,
        [(y * 16 + c * 4 + k, c * 32 + y * 4 + k) for c in range(4) for y in range(8) for k in range(4)],
    )
    bf = lambda a: jnp.asarray(a, BF16)
    return (bf(order), bf(order.T), bf(pick), bf(back), jnp.asarray(near, F32), bf(row_a), bf(row_b), bf(ones), bf(np.eye(256)), bf(slab))


def nt(a, b):
    return lax.dot_general(a, b, (((1,), (1,)), ((), ())), preferred_element_type=F32)


def nn(a, b):
    return jnp.dot(a, b, preferred_element_type=F32)


def moved(table, value):
    return nn(table, value).astype(BF16)


def head_sums(value, ones):
    big = value.astype(BF16)
    small = (value - big.astype(F32)).astype(BF16)
    return nn(big, ones) + nn(small, ones)


def norm_rows(x, gain):
    inverse = lax.rsqrt(jnp.mean(x * x, axis=-1, keepdims=True) + EPS)
    return inverse, (x * inverse * gain).astype(BF16)


def body(tokens, gain, w_qkv, head_scale, w_out, w_merge, d_merged, d_skip,
         order, unorder, pick, back, near_mask, row_a, row_b, ones_t, eye, slab,
         o_skip, o_merged, o_tokens, o_qkv, o_out, o_merge, o_gain, o_scale,
         xk, strips, kv, kvt, st, pt, ptb, dst, q4, da4, keep, hs, hr, rhs, allowed,
         ga, ra1, sa2, ra2, sa3, ra3, sa4, ra4,
         gb, rb1, sb2, rb2, sb3, rb3, sb4, rb4,
         g1, g2, g3, g4, tsem_a, tsem_b, tsem_g, tsem_h):
    near = peers()
    core, x_at, y_at, z_at = (near[a][0] for a in ("core", "x", "y", "z"))
    row, col = lax.axis_index("row"), lax.axis_index("col")
    up, down = (row + ROWS - 1) % ROWS, (row + 1) % ROWS
    left, right = (col + COLS - 1) % COLS, (col + 1) % COLS
    toward = [(down, col), (up, col), (row, right), (row, left), (down, right), (down, left), (up, right), (up, left)]
    reverse = [(up, col), (down, col), (row, left), (row, right), (up, left), (up, right), (down, left), (down, right)]
    bar = pltpu.get_barrier_semaphore()
    for dev in toward:
        pl.semaphore_signal(bar, inc=1, device_id=dev, device_id_type=MESH)
    for axis in ("core", "x", "y", "z"):
        for _, dev in near[axis][1]:
            pl.semaphore_signal(bar, inc=1, device_id=dev, device_id_type=MESH)

    def sems(table, stage):
        return table.at[0, pl.ds(7 * stage, 7)], table.at[1, pl.ds(7 * stage, 7)]

    def halo(stage, devices, sources, targets):
        return start_copies([
            pltpu.make_async_remote_copy(
                src_ref=s, dst_ref=t, send_sem=tsem_h.at[0, 8 * stage + i], recv_sem=tsem_h.at[1, 8 * stage + i],
                device_id=dev, device_id_type=MESH)
            for i, (dev, s, t) in enumerate(zip(devices, sources, targets))
        ])

    strips[...] = moved(pick[...], tokens[...])
    pl.semaphore_wait(bar, 8 + 1 + 3 + 7 + 7)
    spans = [pl.ds(0, 96), pl.ds(96, 96)] + [pl.ds(192 + 16 * s, 16) for s in range(6)]
    ch = halo(
        0, toward,
        [tokens.at[pl.ds(32, 96)], tokens.at[pl.ds(0, 96)]] + [strips.at[pl.ds(16 * s, 16)] for s in range(6)],
        [xk.at[s] for s in spans],
    )

    ones = ones_t[...]
    gains = gain[...]
    lane = lax.broadcasted_iota(jnp.int32, (1, 256), 1) // 64
    scales = jnp.zeros((1, 256), F32)
    for h in range(4):
        scales = jnp.where(lane == h, head_scale[h], scales)
    xp = moved(order[...], tokens[...])
    x = xp.astype(F32)
    inverse, normed = norm_rows(x, gains)
    qkv = nn(normed, w_qkv[...])
    q, k = qkv[:, :256], qkv[:, 256:512]
    q_norm = lax.rsqrt(head_sums(q * q, ones) + EPS)
    k_norm = lax.rsqrt(head_sums(k * k, ones) + EPS)
    q_unit, k_unit = q * q_norm, k * k_norm
    q_hat = (q_unit * scales).astype(BF16)
    keep[0], keep[1], keep[2], keep[3] = q_norm, k_norm, q_unit, k_unit
    kv[:OWN, :256] = k_unit.astype(BF16)
    kv[:OWN, 256:] = qkv[:, 512:].astype(BF16)
    zero = jnp.zeros((), BF16)
    for h in range(4):
        q4[128 * h : 128 * h + 128] = jnp.where(lane == h, q_hat, zero)

    d_group = nt(d_merged[...], w_merge[...])
    d_y = moved(order[...], d_skip[...]).astype(F32) + jnp.concatenate(
        [d_group[:, 256 * g : 256 * g + 256] for g in range(4)], axis=0)
    dy_b = d_y.astype(BF16)
    keep[4] = d_y
    d_attn = nt(dy_b, w_out[...]).astype(BF16)
    for h in range(4):
        da4[128 * h : 128 * h + 128] = jnp.where(lane == h, d_attn, zero)

    yes = lambda c: jnp.where(c, 1.0, 0.0).astype(F32)
    v_up, v_down, v_left, v_right = yes(row > 0), yes(row < ROWS - 1), yes(col > 0), yes(col < COLS - 1)
    factors = [(128, 96, v_up), (224, 96, v_down), (320, 16, v_left), (336, 16, v_right),
               (352, 16, v_up * v_left), (368, 16, v_up * v_right), (384, 16, v_down * v_left), (400, 16, v_down * v_right)]
    allowed[:OWN] = near_mask[:OWN]
    for at, size, f in factors:
        allowed[at : at + size] = near_mask[at : at + size] * f

    wait_copies(ch)
    _, normed_h = norm_rows(xk[...].astype(F32), gains)
    kv_h = nn(normed_h, w_qkv[:, 256:])
    k_h = kv_h[:, :256]
    kv[OWN:, :256] = (k_h * lax.rsqrt(head_sums(k_h * k_h, ones) + EPS)).astype(BF16)
    kv[OWN:, 256:] = kv_h[:, 256:].astype(BF16)

    st[...] = nt(kv[:, :256], q4[...])
    for h in range(4):
        span = slice(128 * h, 128 * h + 128)
        e = jnp.exp(st[:, span]) * allowed[...]
        p = e * (1.0 / jnp.sum(e, axis=0, keepdims=True))
        pt[:, span] = p
        ptb[:, span] = p.astype(BF16)
    kvt[:256] = nt(eye[...], kv[:, :256]).astype(BF16)
    kvt[256:] = nt(eye[...], kv[:, 256:]).astype(BF16)

    def diagonal(full):
        return jnp.concatenate([full[64 * h : 64 * h + 64, 128 * h : 128 * h + 128] for h in range(4)], axis=0).T

    attn = diagonal(nn(kvt[256:], ptb[...])).astype(BF16)
    skip = (x + nn(attn, w_out[...])).astype(BF16)
    dm = d_merged[...]
    for g in range(4):
        part = nn(nt(row_b[...], skip[32 * g : 32 * g + 32]).astype(BF16), dm)
        for c in range(4):
            gb[c, g] = part[:, 128 * c : 128 * c + 128].astype(BF16)
    mine = lambda size, index: pl.ds(pl.multiple_of(index * size, size), size)
    cb = exchange(near["core"][1], lambda t: gb.at[:, :, mine(128, t), :], rb1, *sems(tsem_b, 0))
    o_skip[...] = moved(unorder[...], skip)
    group = jnp.concatenate([skip[32 * g : 32 * g + 32] for g in range(4)], axis=1)
    o_merged[...] = nn(group, w_merge[...]).astype(BF16)

    st[...] = nt(kv[:, 256:], da4[...])
    for h in range(4):
        span = slice(128 * h, 128 * h + 128)
        dw, p = st[:, span], pt[:, span]
        dst[:, span] = (p * (dw - jnp.sum(dw * p, axis=0, keepdims=True))).astype(BF16)
    hs[:, :256] = nn(dst[OWN:], q4[...]).astype(BF16)
    hs[:, 256:] = nn(ptb[OWN:], da4[...]).astype(BF16)
    ch = halo(1, reverse, [hs.at[s] for s in spans], [hr.at[s] for s in spans])

    wait_copies(cb)
    sb2[...] = (gb[:, :, mine(128, core), :].astype(F32) + rb1[0].astype(F32)).astype(BF16)
    cb = exchange(near["x"][1], lambda t: sb2.at[:, :, mine(32, t), :], rb2, *sems(tsem_b, 1))

    d_k = nn(dst[:OWN], q4[...])
    d_v = nn(ptb[:OWN], da4[...])
    d_qhat = diagonal(nn(kvt[:256], dst[...]))
    u = keep[2]
    scale_row = jnp.sum(u * d_qhat, axis=0, keepdims=True)
    g_u = d_qhat * scales
    d_q = (keep[0] * (g_u - u * head_sums(u * g_u, ones))).astype(BF16)
    lhs = jnp.concatenate([nt(row_a[...], normed), nt(row_a[...], attn)], axis=1).astype(BF16)
    rhs[...] = jnp.zeros_like(rhs)
    dy_b = keep[4].astype(BF16)
    for c in range(4):
        rhs[128:, 256 * c + 192 : 256 * c + 256] = dy_b[:, 64 * c : 64 * c + 64]

    wait_copies(ch)
    added = nn(back[...], hr[...])
    d_k = d_k + added[:, :256]
    d_v = d_v + added[:, 256:]
    ku = keep[3]
    d_kraw = (keep[1] * (d_k - ku * head_sums(ku * d_k, ones))).astype(BF16)
    d_qkv = jnp.concatenate([d_q, d_kraw, d_v.astype(BF16)], axis=1)
    for c in range(4):
        rhs[:128, 256 * c : 256 * c + 192] = d_qkv[:, 192 * c : 192 * c + 192]
    for c in range(4):
        ga[c] = nn(lhs, rhs[:, 256 * c : 256 * c + 256]).astype(BF16)
    ca = exchange(near["core"][1], lambda t: rows_at(ga, t, 128), ra1, *sems(tsem_a, 0))

    d_normed = nt(d_qkv, w_qkv[...])
    x = xp.astype(F32)
    gain_row = jnp.sum(x * inverse * d_normed, axis=0, keepdims=True)
    for i, r in enumerate((gain_row[:, :128], gain_row[:, 128:], scale_row[:, :128], scale_row[:, 128:])):
        g1[core, i : i + 1] = r
    g1[core, 4:8] = jnp.zeros((4, 128), F32)
    cg = spread(core, near["core"][1], g1, *sems(tsem_g, 0))

    scaled = gains * d_normed
    g_x = inverse * scaled - x * (inverse * inverse * inverse) * jnp.mean(x * scaled, axis=-1, keepdims=True)
    o_tokens[...] = moved(unorder[...], (keep[4] + g_x).astype(BF16))

    wait_copies(ca)
    sa2[...] = (ga[:, mine(128, core), :].astype(F32) + ra1[0].astype(F32)).astype(BF16)
    ca = exchange(near["x"][1], lambda t: rows_at(sa2, t, 32), ra2, *sems(tsem_a, 1))
    wait_copies(cg)
    g2[x_at] = g1[0] + g1[1]
    cg = spread(x_at, near["x"][1], g2, *sems(tsem_g, 1))
    wait_copies(cb)
    total = sb2[:, :, mine(32, x_at), :].astype(F32)
    for p in range(3):
        total = total + rb2[p].astype(F32)
    sb3[...] = total.astype(BF16)
    cb = exchange(near["y"][1], lambda t: sb3.at[:, t // 2, mine(16, t % 2), :], rb3, *sems(tsem_b, 2))

    wait_copies(ca)
    total = sa2[:, mine(32, x_at), :].astype(F32)
    for p in range(3):
        total = total + ra2[p].astype(F32)
    sa3[...] = moved(slab[...], total.astype(BF16).reshape(128, 256)).reshape(8, 16, 256)
    ca = exchange(near["y"][1], lambda t: sa3.at[t], ra3, *sems(tsem_a, 2))
    wait_copies(cg)
    g3[y_at] = (g2[0] + g2[1]) + (g2[2] + g2[3])
    cg = spread(y_at, near["y"][1], g3, *sems(tsem_g, 2))
    wait_copies(cb)
    total = sb3[:, y_at // 2, mine(16, y_at % 2), :].astype(F32)
    for p in range(7):
        total = total + rb3[p].astype(F32)
    sb4[...] = total
    cb = exchange(near["z"][1], lambda t: sb4.at[t // 2, mine(8, t % 2), :], rb4, *sems(tsem_b, 3))

    wait_copies(ca)
    total = sa3[y_at].astype(F32)
    for p in range(7):
        total = total + ra3[p].astype(F32)
    sa4[...] = total.reshape(2, 8, 256)
    ca = exchange(near["z"][1], lambda t: sa4.at[t // 4], ra4, *sems(tsem_a, 3))
    wait_copies(cg)
    g4[z_at] = ((g3[0] + g3[1]) + (g3[2] + g3[3])) + ((g3[4] + g3[5]) + (g3[6] + g3[7]))
    cg = spread(z_at, near["z"][1], g4, *sems(tsem_g, 3))
    wait_copies(cb)
    total = sb4[z_at // 2, mine(8, z_at % 2), :]
    for p in range(7):
        total = total + rb4[p]
    o_merge[...] = total

    wait_copies(ca)
    total = sa4[z_at // 4]
    for p in range(7):
        total = total + ra4[p]
    part = z_at % 4
    piece = jnp.zeros((2, 256), F32)
    for i in range(4):
        piece = piece + jnp.where(part == i, total[2 * i : 2 * i + 2], 0.0)
    o_qkv[...] = piece[:, :192]
    o_out[...] = piece[:, 192:]
    wait_copies(cg)
    total = ((g4[0] + g4[1]) + (g4[2] + g4[3])) + ((g4[4] + g4[5]) + (g4[6] + g4[7]))
    o_gain[...] = total[0:2]
    halves = lax.broadcasted_iota(jnp.int32, (1, 128), 1)
    out = jnp.zeros((1, 128), F32)
    for h in range(4):
        r = total[2 + h // 2 : 3 + h // 2]
        s = jnp.sum(jnp.where(halves // 64 == h % 2, r, 0.0), axis=1, keepdims=True)
        out = jnp.where(halves == h, s, out)
    o_scale[...] = out


def on_device(tokens, gain, w_qkv, head_scale, w_out, w_merge, d_merged, d_skip):
    V = pltpu.VMEM
    S = jax.ShapeDtypeStruct
    vmem = pl.BlockSpec(memory_space=V)
    smem = pl.BlockSpec(memory_space=pltpu.SMEM)
    DMA = pltpu.SemaphoreType.DMA
    out = pl.pallas_call(
        body,
        out_shape=(
            S((128, 256), BF16), S((32, 512), BF16), S((128, 256), BF16),
            S((2, 192), F32), S((2, 64), F32), S((8, 128), F32), S((2, 128), F32), S((1, 128), F32),
        ),
        in_specs=[vmem] * 3 + [smem] + [vmem] * 14,
        out_specs=(vmem,) * 8,
        scratch_shapes=[
            V((HALO, 256), BF16), V((96, 256), BF16), V((NK, 512), BF16), V((512, NK), BF16),
            V((NK, 512), F32), V((NK, 512), F32), V((NK, 512), BF16), V((NK, 512), BF16),
            V((512, 256), BF16), V((512, 256), BF16), V((5, 128, 256), F32),
            V((HALO, 512), BF16), V((HALO, 512), BF16), V((256, 1024), BF16), V((NK, 128), F32),
            V((4, 256, 256), BF16), V((1, 4, 128, 256), BF16),
            V((4, 128, 256), BF16), V((3, 4, 32, 256), BF16),
            V((8, 16, 256), BF16), V((7, 16, 256), BF16),
            V((2, 8, 256), F32), V((7, 8, 256), F32),
            V((4, 4, 256, 128), BF16), V((1, 4, 4, 128, 128), BF16),
            V((4, 4, 128, 128), BF16), V((3, 4, 4, 32, 128), BF16),
            V((4, 4, 32, 128), BF16), V((7, 4, 16, 128), BF16),
            V((4, 16, 128), F32), V((7, 8, 128), F32),
            V((2, 8, 128), F32), V((4, 8, 128), F32), V((8, 8, 128), F32), V((8, 8, 128), F32),
            DMA((2, 28)), DMA((2, 28)), DMA((2, 28)), DMA((2, 16)),
        ],
        compiler_params=pltpu.CompilerParams(collective_id=0, has_side_effects=True, vmem_limit_bytes=48 * 2**20),
    )(
        tokens.reshape(128, 256), gain.reshape(1, 256), w_qkv, head_scale, w_out, w_merge,
        d_merged.reshape(32, 512), d_skip.reshape(128, 256), *tables(),
    )
    skip, merged, grad, qkv, o, m, g, s = out
    return (skip.reshape(4, 32, 256), merged.reshape(2, 16, 512), grad.reshape(4, 32, 256), qkv, o, m, g.reshape(256), s[0, :4])


def solution(mesh):
    return jax.shard_map(
        on_device,
        mesh=mesh,
        in_specs=(
            P("row", "col", None),
            P(),
            P(),
            P(),
            P(),
            P(),
            P("row", "col", None),
            P("row", "col", None),
        ),
        out_specs=(
            P("row", "col", None),
            P("row", "col", None),
            P("row", "col", None),
            P("row", "col"),
            P("row", "col"),
            P("row", "col"),
            P(),
            P(),
        ),
        check_vma=False,
    )
```

```python
import jax
import jax.numpy as jnp
from jax import lax
from jax.experimental import pallas as pl
from jax.experimental.pallas import tpu as pltpu
from jax.sharding import PartitionSpec as P

EPS = 1e-06
MESH = pl.DeviceIdType.MESH
NX, NY, NZ = 4, 8, 8
ROWS, COLS = 128, 4
F32, BF16 = jnp.float32, jnp.bfloat16
OWN, NK = 128, 416
VMEM_LIMIT = 63 * 2**20
HALO = NK - OWN


def place():
    row, col = lax.axis_index("row"), lax.axis_index("col")
    return row // 16, (row // 8) % 2, (row // 2) % 4, row % 2, col


def device(y, zl, x, core, col):
    return (((y * 2 + zl) * 4 + x) * 2 + core, col)


def peers():
    y, zl, x, core, col = place()
    z = col * 2 + zl
    out = {"core": (core, [(1 - core, device(y, zl, x, 1 - core, col))])}
    out["x"] = (x, [])
    for p in range(1, NX):
        t = (x + p) % NX
        out["x"][1].append((t, device(y, zl, t, core, col)))
    out["y"] = (y, [])
    for p in range(1, NY):
        t = (y + p) % NY
        out["y"][1].append((t, device(t, zl, x, core, col)))
    out["z"] = (z, [])
    for p in range(1, NZ):
        t = (z + p) % NZ
        out["z"][1].append((t, device(y, t % 2, x, core, t // 2)))
    return out


def start_copies(copies):
    for c in copies:
        c.start()
    return copies


def wait_copies(copies):
    for c in copies:
        c.wait()


def exchange(peer_list, source, slots, send, recv):
    return start_copies(
        [
            pltpu.make_async_remote_copy(
                src_ref=source(t),
                dst_ref=slots.at[p],
                send_sem=send.at[p],
                recv_sem=recv.at[p],
                device_id=dev,
                device_id_type=MESH,
            )
            for p, (t, dev) in enumerate(peer_list)
        ]
    )


def spread(mine, peer_list, slots, send, recv):
    return start_copies(
        [
            pltpu.make_async_remote_copy(
                src_ref=slots.at[mine],
                dst_ref=slots.at[mine],
                send_sem=send.at[p],
                recv_sem=recv.at[p],
                device_id=dev,
                device_id_type=MESH,
            )
            for p, (t, dev) in enumerate(peer_list)
        ]
    )


def rows_at(ref, index, size):
    return ref.at[:, pl.ds(pl.multiple_of(index * size, size), size), :]


def along(axis, size):
    return lax.broadcasted_iota(jnp.int32, (size, 1) if axis == 0 else (1, size), axis)


def token_of(p):
    return ((((p >> 4) & 1) * 2 + (p >> 6)) << 5) + (p & 15) * 2 + ((p >> 5) & 1)


def place_of(t):
    r, c = t >> 5, t & 31
    return ((r & 1) * 2 + (c & 1)) * 32 + (r >> 1) * 16 + (c >> 1)


def third(k):
    return (k * 11) >> 5


def slot_token(i):
    s, k = i >> 4, i & 15
    r = third(k) + jnp.where((s == 2) | (s == 3), 1, 0)
    c = k - 3 * third(k) + jnp.where((s & 1) == 0, 29, 0)
    return jnp.where(k < jnp.where(s < 2, 12, 9), r * 32 + c, -1)


def sent_token(k):
    return jnp.where(k < 96, k + 32, jnp.where(k < 192, k - 96, slot_token(k - 192)))


def row_a_of(n):
    return ((((n >> 2) & 7) * 2 + ((n >> 1) & 1)) * 4 + ((n >> 5) & 3)) * 4 + (n >> 7) * 2 + (n & 1)


def row_b_of(n):
    return ((n >> 4) & 1) * 128 + ((n >> 3) & 1) * 64 + ((n >> 5) & 3) * 16 + (n >> 7) * 8 + (n & 7)


def slab_of(n):
    return ((n >> 2) & 3) * 32 + (n >> 4) * 4 + (n & 3)


def one_hot(rows, cols):
    return jnp.where(rows == cols, 1.0, 0.0).astype(BF16)


def allowed_keys(row, col):
    n, p = along(0, NK), along(1, 128)
    own = token_of(n)
    i = n - 320
    s, k = i >> 4, i & 15
    slot_r = third(k) + jnp.where(s < 2, 0, jnp.where(s < 4, -3, 4))
    slot_c = k - 3 * third(k) + jnp.where((s & 1) == 0, -3, 32)
    slot_r = jnp.where(k < jnp.where(s < 2, 12, 9), slot_r, 1000)
    side = jnp.where(n < 224, n - 128, n - 224)
    kr = jnp.where(n < 128, own >> 5, jnp.where(n < 320, (side >> 5) + jnp.where(n < 224, -3, 4), slot_r))
    kc = jnp.where(n < 128, own & 31, jnp.where(n < 320, side & 31, slot_c))
    inside = (kr + 4 * row >= 0) & (kr + 4 * row < 4 * ROWS) & (kc + 32 * col >= 0) & (kc + 32 * col < 32 * COLS)
    kr = jnp.where(inside, kr, 1000)
    query = token_of(p)
    return jnp.where((jnp.abs(kr - (query >> 5)) <= 3) & (jnp.abs(kc - (query & 31)) <= 3), 1.0, 0.0)


def nt(a, b):
    return lax.dot_general(a, b, (((1,), (1,)), ((), ())), preferred_element_type=F32)


def nn(a, b):
    return jnp.dot(a, b, preferred_element_type=F32)


def moved(table, value):
    return nn(table, value).astype(BF16)


def head_sums(value, ones):
    big = value.astype(BF16)
    small = (value - big.astype(F32)).astype(BF16)
    return nn(big, ones) + nn(small, ones)


def norm_rows(x, gain):
    inverse = lax.rsqrt(jnp.mean(x * x, axis=-1, keepdims=True) + EPS)
    return inverse, (x * inverse * gain).astype(BF16)


def body(*refs):
    sources, targets, held, ready, (load_sem, save_sem), work = (
        refs[:8], refs[8:16], refs[16:24], refs[24:32], refs[32:34], refs[34:])
    loads = [pltpu.make_async_copy(s, t, load_sem.at[i]) for i, (s, t) in enumerate(zip(sources, held))]
    saves = [pltpu.make_async_copy(s, t, save_sem.at[i]) for i, (s, t) in enumerate(zip(ready, targets))]
    for i in FIRST:
        loads[i].start()
    compute(loads, saves, *held, *ready, *work)


FIRST = (0, 2, 1, 3, 6, 7, 5, 4)


def compute(loads, saves, tokens, gain, w_qkv, head_scale, w_out, w_merge, d_merged, d_skip,
         o_skip, o_merged, o_tokens, o_qkv, o_out, o_merge, o_gain, o_scale,
         xk, strips, row_a, row_b, ones_t, kv, kvt, st, pt, ptb, dst, q4, da4, keep, hs, hr, rhs, allowed,
         ga, ra1, sa2, ra2, sa3, ra3, sa4, ra4,
         gb, rb1, sb2, rb2, sb3, rb3, sb4, rb4,
         g1, g2, g3, g4, tsem_a, tsem_b, tsem_g, tsem_h):
    near = peers()
    core, x_at, y_at, z_at = (near[a][0] for a in ("core", "x", "y", "z"))
    row, col = lax.axis_index("row"), lax.axis_index("col")
    up, down = (row + ROWS - 1) % ROWS, (row + 1) % ROWS
    left, right = (col + COLS - 1) % COLS, (col + 1) % COLS
    toward = [(down, col), (up, col), (row, right), (row, left), (down, right), (down, left), (up, right), (up, left)]
    reverse = [(up, col), (down, col), (row, left), (row, right), (up, left), (up, right), (down, left), (down, right)]
    bar = pltpu.get_barrier_semaphore()
    for dev in toward:
        pl.semaphore_signal(bar, inc=1, device_id=dev, device_id_type=MESH)
    for axis in ("core", "x", "y", "z"):
        for _, dev in near[axis][1]:
            pl.semaphore_signal(bar, inc=1, device_id=dev, device_id_type=MESH)

    def sems(table, stage):
        return table.at[0, pl.ds(7 * stage, 7)], table.at[1, pl.ds(7 * stage, 7)]

    def halo(stage, devices, sources, targets):
        return start_copies([
            pltpu.make_async_remote_copy(
                src_ref=s, dst_ref=t, send_sem=tsem_h.at[0, 8 * stage + i], recv_sem=tsem_h.at[1, 8 * stage + i],
                device_id=dev, device_id_type=MESH)
            for i, (dev, s, t) in enumerate(zip(devices, sources, targets))
        ])

    def loaded(*names):
        for i in names:
            loads[i].wait()

    token_row = along(1, 128)
    pick = one_hot(slot_token(along(0, 96)), token_row)
    loaded(0)
    strips[...] = moved(pick, tokens[...])
    order = one_hot(token_of(along(0, 128)), token_row)
    feature = along(1, 256)
    row_a[...] = one_hot(row_a_of(along(0, 256)), feature)
    row_b[...] = one_hot(row_b_of(along(0, 256)), feature)
    ones_t[...] = one_hot(along(0, 256) >> 6, feature >> 6)
    allowed[...] = allowed_keys(row, col)
    rhs[...] = jnp.zeros_like(rhs)
    pl.semaphore_wait(bar, 8 + 1 + 3 + 7 + 7)
    spans = [pl.ds(0, 96), pl.ds(96, 96)] + [pl.ds(192 + 16 * s, 16) for s in range(6)]
    ch = halo(
        0, toward,
        [tokens.at[pl.ds(32, 96)], tokens.at[pl.ds(0, 96)]] + [strips.at[pl.ds(16 * s, 16)] for s in range(6)],
        [xk.at[s] for s in spans],
    )

    loaded(1, 2, 3)
    ones = ones_t[...]
    gains = gain[...]
    lane = lax.broadcasted_iota(jnp.int32, (1, 256), 1) // 64
    scales = jnp.zeros((1, 256), F32)
    for h in range(4):
        scales = jnp.where(lane == h, head_scale[:, h : h + 1], scales)
    xp = moved(order, tokens[...])
    x = xp.astype(F32)
    inverse, normed = norm_rows(x, gains)
    qkv = nn(normed, w_qkv[...])
    q, k = qkv[:, :256], qkv[:, 256:512]
    q_norm = lax.rsqrt(head_sums(q * q, ones) + EPS)
    k_norm = lax.rsqrt(head_sums(k * k, ones) + EPS)
    q_unit, k_unit = q * q_norm, k * k_norm
    q_hat = (q_unit * scales).astype(BF16)
    keep[0], keep[1], keep[2], keep[3] = q_norm, k_norm, q_unit, k_unit
    kv[:OWN, :256] = k_unit.astype(BF16)
    kv[:OWN, 256:] = qkv[:, 512:].astype(BF16)
    zero = jnp.zeros((), BF16)
    for h in range(4):
        q4[128 * h : 128 * h + 128] = jnp.where(lane == h, q_hat, zero)

    loaded(4, 5, 6, 7)
    d_group = nt(d_merged[...], w_merge[...])
    d_y = moved(order, d_skip[...]).astype(F32) + jnp.concatenate(
        [d_group[:, 256 * g : 256 * g + 256] for g in range(4)], axis=0)
    dy_b = d_y.astype(BF16)
    keep[4] = d_y
    d_attn = nt(dy_b, w_out[...]).astype(BF16)
    for h in range(4):
        da4[128 * h : 128 * h + 128] = jnp.where(lane == h, d_attn, zero)

    wait_copies(ch)
    _, normed_h = norm_rows(xk[...].astype(F32), gains)
    kv_h = nn(normed_h, w_qkv[:, 256:])
    k_h = kv_h[:, :256]
    kv[OWN:, :256] = (k_h * lax.rsqrt(head_sums(k_h * k_h, ones) + EPS)).astype(BF16)
    kv[OWN:, 256:] = kv_h[:, 256:].astype(BF16)

    st[...] = nt(kv[:, :256], q4[...])
    for h in range(4):
        span = slice(128 * h, 128 * h + 128)
        e = jnp.exp(st[:, span]) * allowed[...]
        p = e * (1.0 / jnp.sum(e, axis=0, keepdims=True))
        pt[:, span] = p
        ptb[:, span] = p.astype(BF16)
    eye = one_hot(along(0, 256), feature)
    kvt[:256] = nt(eye, kv[:, :256]).astype(BF16)
    kvt[256:] = nt(eye, kv[:, 256:]).astype(BF16)

    def diagonal(full):
        return jnp.concatenate([full[64 * h : 64 * h + 64, 128 * h : 128 * h + 128] for h in range(4)], axis=0).T

    attn = diagonal(nn(kvt[256:], ptb[...])).astype(BF16)
    skip = (x + nn(attn, w_out[...])).astype(BF16)
    dm = d_merged[...]
    for g in range(4):
        part = nn(nt(row_b[...], skip[32 * g : 32 * g + 32]).astype(BF16), dm)
        for c in range(4):
            gb[c, g] = part[:, 128 * c : 128 * c + 128].astype(BF16)
    mine = lambda size, index: pl.ds(pl.multiple_of(index * size, size), size)
    cb = exchange(near["core"][1], lambda t: gb.at[:, :, mine(128, t), :], rb1, *sems(tsem_b, 0))
    o_skip[...] = moved(one_hot(place_of(along(0, 128)), token_row), skip)
    group = jnp.concatenate([skip[32 * g : 32 * g + 32] for g in range(4)], axis=1)
    o_merged[...] = nn(group, w_merge[...]).astype(BF16)
    saves[0].start()
    saves[1].start()

    st[...] = nt(kv[:, 256:], da4[...])
    for h in range(4):
        span = slice(128 * h, 128 * h + 128)
        dw, p = st[:, span], pt[:, span]
        dst[:, span] = (p * (dw - jnp.sum(dw * p, axis=0, keepdims=True))).astype(BF16)
    hs[:, :256] = nn(dst[OWN:], q4[...]).astype(BF16)
    hs[:, 256:] = nn(ptb[OWN:], da4[...]).astype(BF16)
    ch = halo(1, reverse, [hs.at[s] for s in spans], [hr.at[s] for s in spans])

    wait_copies(cb)
    sb2[...] = (gb[:, :, mine(128, core), :].astype(F32) + rb1[0].astype(F32)).astype(BF16)
    cb = exchange(near["x"][1], lambda t: sb2.at[:, :, mine(32, t), :], rb2, *sems(tsem_b, 1))

    d_k = nn(dst[:OWN], q4[...])
    d_v = nn(ptb[:OWN], da4[...])
    d_qhat = diagonal(nn(kvt[:256], dst[...]))
    u = keep[2]
    scale_row = jnp.sum(u * d_qhat, axis=0, keepdims=True)
    g_u = d_qhat * scales
    d_q = (keep[0] * (g_u - u * head_sums(u * g_u, ones))).astype(BF16)
    lhs = jnp.concatenate([nt(row_a[...], normed), nt(row_a[...], attn)], axis=1).astype(BF16)
    dy_b = keep[4].astype(BF16)
    for c in range(4):
        rhs[128:, 256 * c + 192 : 256 * c + 256] = dy_b[:, 64 * c : 64 * c + 64]

    wait_copies(ch)
    added = nn(one_hot(token_of(along(0, 128)), sent_token(along(1, HALO))), hr[...])
    d_k = d_k + added[:, :256]
    d_v = d_v + added[:, 256:]
    ku = keep[3]
    d_kraw = (keep[1] * (d_k - ku * head_sums(ku * d_k, ones))).astype(BF16)
    d_qkv = jnp.concatenate([d_q, d_kraw, d_v.astype(BF16)], axis=1)
    for c in range(4):
        rhs[:128, 256 * c : 256 * c + 192] = d_qkv[:, 192 * c : 192 * c + 192]
    for c in range(4):
        ga[c] = nn(lhs, rhs[:, 256 * c : 256 * c + 256]).astype(BF16)
    ca = exchange(near["core"][1], lambda t: rows_at(ga, t, 128), ra1, *sems(tsem_a, 0))

    d_normed = nt(d_qkv, w_qkv[...])
    x = xp.astype(F32)
    gain_row = jnp.sum(x * inverse * d_normed, axis=0, keepdims=True)
    for i, r in enumerate((gain_row[:, :128], gain_row[:, 128:], scale_row[:, :128], scale_row[:, 128:])):
        g1[core, i : i + 1] = r
    g1[core, 4:8] = jnp.zeros((4, 128), F32)
    cg = spread(core, near["core"][1], g1, *sems(tsem_g, 0))

    scaled = gains * d_normed
    g_x = inverse * scaled - x * (inverse * inverse * inverse) * jnp.mean(x * scaled, axis=-1, keepdims=True)
    o_tokens[...] = moved(one_hot(place_of(along(0, 128)), token_row), (keep[4] + g_x).astype(BF16))
    saves[2].start()

    wait_copies(ca)
    sa2[...] = (ga[:, mine(128, core), :].astype(F32) + ra1[0].astype(F32)).astype(BF16)
    ca = exchange(near["x"][1], lambda t: rows_at(sa2, t, 32), ra2, *sems(tsem_a, 1))
    wait_copies(cg)
    g2[x_at] = g1[0] + g1[1]
    cg = spread(x_at, near["x"][1], g2, *sems(tsem_g, 1))
    wait_copies(cb)
    total = sb2[:, :, mine(32, x_at), :].astype(F32)
    for p in range(3):
        total = total + rb2[p].astype(F32)
    sb3[...] = total.astype(BF16)
    cb = exchange(near["y"][1], lambda t: sb3.at[:, t // 2, mine(16, t % 2), :], rb3, *sems(tsem_b, 2))

    wait_copies(ca)
    total = sa2[:, mine(32, x_at), :].astype(F32)
    for p in range(3):
        total = total + ra2[p].astype(F32)
    sa3[...] = moved(one_hot(slab_of(along(0, 128)), token_row), total.astype(BF16).reshape(128, 256)).reshape(8, 16, 256)
    ca = exchange(near["y"][1], lambda t: sa3.at[t], ra3, *sems(tsem_a, 2))
    wait_copies(cg)
    g3[y_at] = (g2[0] + g2[1]) + (g2[2] + g2[3])
    cg = spread(y_at, near["y"][1], g3, *sems(tsem_g, 2))
    wait_copies(cb)
    total = sb3[:, y_at // 2, mine(16, y_at % 2), :].astype(F32)
    for p in range(7):
        total = total + rb3[p].astype(F32)
    sb4[...] = total
    cb = exchange(near["z"][1], lambda t: sb4.at[t // 2, mine(8, t % 2), :], rb4, *sems(tsem_b, 3))

    wait_copies(ca)
    total = sa3[y_at].astype(F32)
    for p in range(7):
        total = total + ra3[p].astype(F32)
    sa4[...] = total.reshape(2, 8, 256)
    ca = exchange(near["z"][1], lambda t: sa4.at[t // 4], ra4, *sems(tsem_a, 3))
    wait_copies(cg)
    g4[z_at] = ((g3[0] + g3[1]) + (g3[2] + g3[3])) + ((g3[4] + g3[5]) + (g3[6] + g3[7]))
    cg = spread(z_at, near["z"][1], g4, *sems(tsem_g, 3))
    wait_copies(cb)
    total = sb4[z_at // 2, mine(8, z_at % 2), :]
    for p in range(7):
        total = total + rb4[p]
    o_merge[...] = total
    saves[5].start()

    wait_copies(ca)
    total = sa4[z_at // 4]
    for p in range(7):
        total = total + ra4[p]
    part = z_at % 4
    piece = jnp.zeros((2, 256), F32)
    for i in range(4):
        piece = piece + jnp.where(part == i, total[2 * i : 2 * i + 2], 0.0)
    o_qkv[...] = piece[:, :192]
    o_out[...] = piece[:, 192:]
    saves[3].start()
    saves[4].start()
    wait_copies(cg)
    total = ((g4[0] + g4[1]) + (g4[2] + g4[3])) + ((g4[4] + g4[5]) + (g4[6] + g4[7]))
    o_gain[...] = total[0:2]
    halves = lax.broadcasted_iota(jnp.int32, (1, 128), 1)
    out = jnp.zeros((1, 128), F32)
    for h in range(4):
        r = total[2 + h // 2 : 3 + h // 2]
        s = jnp.sum(jnp.where(halves // 64 == h % 2, r, 0.0), axis=1, keepdims=True)
        out = jnp.where(halves == h, s, out)
    o_scale[...] = out[:, :4]
    saves[6].start()
    saves[7].start()
    wait_copies(saves)


def hand_over(*refs):
    sources, targets, sem = refs[:8], refs[8:16], refs[16]
    wait_copies(start_copies(
        [pltpu.make_async_copy(s, t, sem.at[i]) for i, (s, t) in enumerate(zip(sources, targets))]))


def on_device(tokens, gain, w_qkv, head_scale, w_out, w_merge, d_merged, d_skip):
    V = pltpu.VMEM
    S = jax.ShapeDtypeStruct
    DMA = pltpu.SemaphoreType.DMA
    operands = (
        tokens.reshape(128, 256), gain.reshape(1, 256), w_qkv, head_scale.reshape(1, 4), w_out, w_merge,
        d_merged.reshape(32, 512), d_skip.reshape(128, 256),
    )
    results = (
        S((128, 256), BF16), S((32, 512), BF16), S((128, 256), BF16),
        S((2, 192), F32), S((2, 64), F32), S((8, 128), F32), S((2, 128), F32), S((1, 4), F32),
    )
    far = pl.BlockSpec(memory_space=pltpu.MemorySpace.HBM)
    out = pl.pallas_call(
        body,
        out_shape=results,
        in_specs=[far] * 8,
        out_specs=(far,) * 8,
        scratch_shapes=[V(a.shape, a.dtype) for a in operands + results] + [
            DMA((8,)), DMA((8,)),
            V((HALO, 256), BF16), V((96, 256), BF16), V((256, 256), BF16), V((256, 256), BF16), V((256, 256), BF16), V((NK, 512), BF16), V((512, NK), BF16),
            V((NK, 512), F32), V((NK, 512), F32), V((NK, 512), BF16), V((NK, 512), BF16),
            V((512, 256), BF16), V((512, 256), BF16), V((5, 128, 256), F32),
            V((HALO, 512), BF16), V((HALO, 512), BF16), V((256, 1024), BF16), V((NK, 128), F32),
            V((4, 256, 256), BF16), V((1, 4, 128, 256), BF16),
            V((4, 128, 256), BF16), V((3, 4, 32, 256), BF16),
            V((8, 16, 256), BF16), V((7, 16, 256), BF16),
            V((2, 8, 256), F32), V((7, 8, 256), F32),
            V((4, 4, 256, 128), BF16), V((1, 4, 4, 128, 128), BF16),
            V((4, 4, 128, 128), BF16), V((3, 4, 4, 32, 128), BF16),
            V((4, 4, 32, 128), BF16), V((7, 4, 16, 128), BF16),
            V((4, 16, 128), F32), V((7, 8, 128), F32),
            V((2, 8, 128), F32), V((4, 8, 128), F32), V((8, 8, 128), F32), V((8, 8, 128), F32),
            DMA((2, 28)), DMA((2, 28)), DMA((2, 28)), DMA((2, 16)),
        ],
        compiler_params=pltpu.CompilerParams(collective_id=0, has_side_effects=True, vmem_limit_bytes=VMEM_LIMIT),
    )(*operands)
    out = pl.pallas_call(
        hand_over,
        out_shape=results,
        in_specs=[far] * 8,
        out_specs=(far,) * 8,
        scratch_shapes=[DMA((8,))],
        compiler_params=pltpu.CompilerParams(vmem_limit_bytes=VMEM_LIMIT),
    )(*out)
    skip, merged, grad, qkv, o, m, g, s = out
    return (skip.reshape(4, 32, 256), merged.reshape(2, 16, 512), grad.reshape(4, 32, 256), qkv, o, m, g.reshape(256), s.reshape(4))


def solution(mesh):
    return jax.shard_map(
        on_device,
        mesh=mesh,
        in_specs=(
            P("row", "col", None),
            P(),
            P(),
            P(),
            P(),
            P(),
            P("row", "col", None),
            P("row", "col", None),
        ),
        out_specs=(
            P("row", "col", None),
            P("row", "col", None),
            P("row", "col", None),
            P("row", "col"),
            P("row", "col"),
            P("row", "col"),
            P(),
            P(),
        ),
        check_vma=False,
    )
```

```python
import jax
import jax.numpy as jnp
from jax import lax
from jax.experimental import pallas as pl
from jax.experimental.pallas import tpu as pltpu
from jax.sharding import PartitionSpec as P

EPS = 1e-06
MESH = pl.DeviceIdType.MESH
NX, NY, NZ = 4, 8, 8
ROWS, COLS = 128, 4
F32, BF16 = jnp.float32, jnp.bfloat16
OWN, NK = 128, 416
VMEM_LIMIT = 63 * 2**20
HALO = NK - OWN


def place():
    row, col = lax.axis_index("row"), lax.axis_index("col")
    return row // 16, (row // 8) % 2, (row // 2) % 4, row % 2, col


def device(y, zl, x, core, col):
    return (((y * 2 + zl) * 4 + x) * 2 + core, col)


def peers():
    y, zl, x, core, col = place()
    z = col * 2 + zl
    out = {"core": (core, [(1 - core, device(y, zl, x, 1 - core, col))])}
    out["x"] = (x, [])
    for p in range(1, NX):
        t = (x + p) % NX
        out["x"][1].append((t, device(y, zl, t, core, col)))
    out["y"] = (y, [])
    for p in range(1, NY):
        t = (y + p) % NY
        out["y"][1].append((t, device(t, zl, x, core, col)))
    out["z"] = (z, [])
    for p in range(1, NZ):
        t = (z + p) % NZ
        out["z"][1].append((t, device(y, t % 2, x, core, t // 2)))
    return out


def start_copies(copies):
    for c in copies:
        c.start()
    return copies


def wait_copies(copies):
    for c in copies:
        c.wait()


def exchange(peer_list, source, slots, send, recv):
    return start_copies(
        [
            pltpu.make_async_remote_copy(
                src_ref=source(t),
                dst_ref=slots.at[p],
                send_sem=send.at[p],
                recv_sem=recv.at[p],
                device_id=dev,
                device_id_type=MESH,
            )
            for p, (t, dev) in enumerate(peer_list)
        ]
    )


def spread(mine, peer_list, slots, send, recv):
    return start_copies(
        [
            pltpu.make_async_remote_copy(
                src_ref=slots.at[mine],
                dst_ref=slots.at[mine],
                send_sem=send.at[p],
                recv_sem=recv.at[p],
                device_id=dev,
                device_id_type=MESH,
            )
            for p, (t, dev) in enumerate(peer_list)
        ]
    )


def along(axis, size):
    return lax.broadcasted_iota(jnp.int32, (size, 1) if axis == 0 else (1, size), axis)


def token_of(p):
    return ((((p >> 4) & 1) * 2 + (p >> 6)) << 5) + (p & 15) * 2 + ((p >> 5) & 1)


def place_of(t):
    r, c = t >> 5, t & 31
    return ((r & 1) * 2 + (c & 1)) * 32 + (r >> 1) * 16 + (c >> 1)


def third(k):
    return (k * 11) >> 5


def slot_token(i):
    s, k = i >> 4, i & 15
    r = third(k) + jnp.where((s == 2) | (s == 3), 1, 0)
    c = k - 3 * third(k) + jnp.where((s & 1) == 0, 29, 0)
    return jnp.where(k < jnp.where(s < 2, 12, 9), r * 32 + c, -1)


def sent_token(k):
    return jnp.where(k < 96, k + 32, jnp.where(k < 192, k - 96, slot_token(k - 192)))


def row_a_of(n):
    return ((((n >> 2) & 7) * 2 + ((n >> 1) & 1)) * 4 + ((n >> 5) & 3)) * 4 + (n >> 7) * 2 + (n & 1)


def row_b_of(n):
    return ((n >> 3) & 1) * 64 + ((n >> 4) & 3) * 16 + (n >> 6) * 8 + (n & 7)


def slab_of(n):
    return ((n >> 2) & 3) * 32 + (n >> 4) * 4 + (n & 3)


def one_hot(rows, cols):
    return jnp.where(rows == cols, 1.0, 0.0).astype(BF16)


def allowed_keys(row, col):
    n, p = along(0, NK), along(1, 128)
    own = token_of(n)
    i = n - 320
    s, k = i >> 4, i & 15
    slot_r = third(k) + jnp.where(s < 2, 0, jnp.where(s < 4, -3, 4))
    slot_c = k - 3 * third(k) + jnp.where((s & 1) == 0, -3, 32)
    slot_r = jnp.where(k < jnp.where(s < 2, 12, 9), slot_r, 1000)
    side = jnp.where(n < 224, n - 128, n - 224)
    kr = jnp.where(n < 128, own >> 5, jnp.where(n < 320, (side >> 5) + jnp.where(n < 224, -3, 4), slot_r))
    kc = jnp.where(n < 128, own & 31, jnp.where(n < 320, side & 31, slot_c))
    inside = (kr + 4 * row >= 0) & (kr + 4 * row < 4 * ROWS) & (kc + 32 * col >= 0) & (kc + 32 * col < 32 * COLS)
    kr = jnp.where(inside, kr, 1000)
    query = token_of(p)
    return jnp.where((jnp.abs(kr - (query >> 5)) <= 3) & (jnp.abs(kc - (query & 31)) <= 3), 1.0, 0.0)


def nt(a, b):
    return lax.dot_general(a, b, (((1,), (1,)), ((), ())), preferred_element_type=F32)


def nn(a, b):
    return jnp.dot(a, b, preferred_element_type=F32)


def moved(table, value):
    return nn(table, value).astype(BF16)


def head_sums(value, ones):
    big = value.astype(BF16)
    small = (value - big.astype(F32)).astype(BF16)
    return nn(big, ones) + nn(small, ones)


def norm_rows(x, gain):
    inverse = lax.rsqrt(jnp.mean(x * x, axis=-1, keepdims=True) + EPS)
    return inverse, (x * inverse * gain).astype(BF16)


def body(*refs):
    sources, targets, held, ready, (load_sem, save_sem), work = (
        refs[:8], refs[8:16], refs[16:24], refs[24:32], refs[32:34], refs[34:])
    loads = [pltpu.make_async_copy(s, t, load_sem.at[i]) for i, (s, t) in enumerate(zip(sources, held))]
    saves = [pltpu.make_async_copy(s, t, save_sem.at[i]) for i, (s, t) in enumerate(zip(ready, targets))]
    for i in FIRST:
        loads[i].start()
    compute(loads, saves, *held, *ready, *work)


FIRST = (0, 2, 1, 3, 6, 7, 5, 4)


def compute(loads, saves, tokens, gain, w_qkv, head_scale, w_out, w_merge, d_merged, d_skip,
         o_skip, o_merged, o_tokens, o_qkv, o_out, o_merge, o_gain, o_scale,
         xk, strips, row_a, row_b, ones_t, kv, kvt, st, pt, ptb, dst, q4, da4, keep, keys, xhat, nt_all, hs, hr, allowed,
         ga, ra1, sa2, ra2, sa3, ra3, sa4, ra4,
         skips, gx, dmx, gb, rb1, sb2, rb2, sb4, rb4,
         g1, g2, g3, g4, tsem_a, tsem_b, tsem_d, tsem_g, tsem_h):
    near = peers()
    core, x_at, y_at, z_at = (near[a][0] for a in ("core", "x", "y", "z"))
    row, col = lax.axis_index("row"), lax.axis_index("col")
    up, down = (row + ROWS - 1) % ROWS, (row + 1) % ROWS
    left, right = (col + COLS - 1) % COLS, (col + 1) % COLS
    toward = [(down, col), (up, col), (row, right), (row, left), (down, right), (down, left), (up, right), (up, left)]
    reverse = [(up, col), (down, col), (row, left), (row, right), (up, left), (up, right), (down, left), (down, right)]
    bar = pltpu.get_barrier_semaphore()
    for dev in toward:
        pl.semaphore_signal(bar, inc=1, device_id=dev, device_id_type=MESH)
    for axis in ("core", "x", "y", "z"):
        for _, dev in near[axis][1]:
            pl.semaphore_signal(bar, inc=1, device_id=dev, device_id_type=MESH)

    def sems(table, stage):
        return table.at[0, pl.ds(7 * stage, 7)], table.at[1, pl.ds(7 * stage, 7)]

    def halo(stage, devices, sources, targets):
        return start_copies([
            pltpu.make_async_remote_copy(
                src_ref=s, dst_ref=t, send_sem=tsem_h.at[0, 8 * stage + i], recv_sem=tsem_h.at[1, 8 * stage + i],
                device_id=dev, device_id_type=MESH)
            for i, (dev, s, t) in enumerate(zip(devices, sources, targets))
        ])

    def loaded(*names):
        for i in names:
            loads[i].wait()

    token_row = along(1, 128)
    pick = one_hot(slot_token(along(0, 96)), token_row)
    loaded(0)
    strips[...] = moved(pick, tokens[...])
    order = one_hot(token_of(along(0, 128)), token_row)
    feature = along(1, 256)
    row_a[...] = one_hot(row_a_of(along(0, 256)), feature)
    row_b[...] = one_hot(row_b_of(along(0, 128)), token_row)
    ones_t[...] = one_hot(along(0, 256) >> 6, feature >> 6)
    allowed[...] = allowed_keys(row, col)
    pl.semaphore_wait(bar, 8 + 1 + 3 + 7 + 7)
    spans = [pl.ds(0, 96), pl.ds(96, 96)] + [pl.ds(192 + 16 * s, 16) for s in range(6)]
    ch = halo(
        0, toward,
        [tokens.at[pl.ds(32, 96)], tokens.at[pl.ds(0, 96)]] + [strips.at[pl.ds(16 * s, 16)] for s in range(6)],
        [xk.at[s] for s in spans],
    )

    loaded(6)
    dmx[7] = d_merged[...]
    cd = exchange(near["y"][1], lambda t: d_merged, dmx, tsem_d.at[0], tsem_d.at[1])

    loaded(1, 2, 3)
    ones = ones_t[...]
    gains = gain[...]
    lane = lax.broadcasted_iota(jnp.int32, (1, 256), 1) // 64
    scales = jnp.zeros((1, 256), F32)
    for h in range(4):
        scales = jnp.where(lane == h, head_scale[:, h : h + 1], scales)
    xp = moved(order, tokens[...])
    x = xp.astype(F32)
    inverse, normed = norm_rows(x, gains)
    xhat[:OWN] = x * inverse
    nt_all[:, :OWN] = nt(row_a[...], normed).astype(BF16)
    qkv = nn(normed, w_qkv[...])
    q, k = qkv[:, :256], qkv[:, 256:512]
    q_norm = lax.rsqrt(head_sums(q * q, ones) + EPS)
    k_norm = lax.rsqrt(head_sums(k * k, ones) + EPS)
    q_unit, k_unit = q * q_norm, k * k_norm
    q_hat = (q_unit * scales).astype(BF16)
    keep[0], keep[1] = q_norm, q_unit
    keys[0, :OWN], keys[1, :OWN] = k_norm, k_unit
    kv[:OWN, :256] = k_unit.astype(BF16)
    kv[:OWN, 256:] = qkv[:, 512:].astype(BF16)
    zero = jnp.zeros((), BF16)
    for h in range(4):
        q4[128 * h : 128 * h + 128] = jnp.where(lane == h, q_hat, zero)

    loaded(4, 5, 7)
    d_group = nt(d_merged[...], w_merge[...])
    d_y = moved(order, d_skip[...]).astype(F32) + jnp.concatenate(
        [d_group[:, 256 * g : 256 * g + 256] for g in range(4)], axis=0)
    dy_b = d_y.astype(BF16)
    keep[2] = d_y
    d_attn = nt(dy_b, w_out[...]).astype(BF16)
    for h in range(4):
        da4[128 * h : 128 * h + 128] = jnp.where(lane == h, d_attn, zero)

    wait_copies(ch)
    xh = xk[...].astype(F32)
    inverse_h, normed_h = norm_rows(xh, gains)
    kv_h = nn(normed_h, w_qkv[:, 256:])
    k_h = kv_h[:, :256]
    k_norm_h = lax.rsqrt(head_sums(k_h * k_h, ones) + EPS)
    k_unit_h = k_h * k_norm_h
    keys[0, OWN:], keys[1, OWN:] = k_norm_h, k_unit_h
    kv[OWN:, :256] = k_unit_h.astype(BF16)
    kv[OWN:, 256:] = kv_h[:, 256:].astype(BF16)

    st[...] = nt(kv[:, :256], q4[...])
    for h in range(4):
        span = slice(128 * h, 128 * h + 128)
        e = jnp.exp(st[:, span]) * allowed[...]
        p = e * (1.0 / jnp.sum(e, axis=0, keepdims=True))
        pt[:, span] = p
        ptb[:, span] = p.astype(BF16)

    st[...] = nt(kv[:, 256:], da4[...])
    for h in range(4):
        span = slice(128 * h, 128 * h + 128)
        dw, p = st[:, span], pt[:, span]
        dst[:, span] = (p * (dw - jnp.sum(dw * p, axis=0, keepdims=True))).astype(BF16)
    d_k = nn(dst[...], q4[...])
    ku = keys[1]
    d_kraw = (keys[0] * (d_k - ku * head_sums(ku * d_k, ones))).astype(BF16)
    d_v = nn(ptb[...], da4[...]).astype(BF16)
    nt_all[:, OWN:] = nt(row_a[...], normed_h).astype(BF16)
    normed_t = nt_all[...]
    eye = one_hot(along(0, 256), feature)
    kvt[:256] = nt(eye, kv[:, :256]).astype(BF16)
    kvt[256:] = nt(eye, kv[:, 256:]).astype(BF16)

    def diagonal(full):
        return jnp.concatenate([full[64 * h : 64 * h + 64, 128 * h : 128 * h + 128] for h in range(4)], axis=0)

    d_qhat = diagonal(nn(kvt[:256], dst[...])).T
    u = keep[1]
    g_u = d_qhat * scales
    d_q = (keep[0] * (g_u - u * head_sums(u * g_u, ones))).astype(BF16)
    attn_t = diagonal(nn(kvt[256:], ptb[...]))
    ga[:, :256] = nn(normed_t[:, :OWN], d_q).astype(BF16)
    ga[:, 256:512] = nn(normed_t, d_kraw).astype(BF16)
    ga[:, 512:768] = nn(normed_t, d_v).astype(BF16)
    ga[:, 768:] = nn(nn(row_a[...], attn_t.astype(BF16)).astype(BF16), keep[2].astype(BF16)).astype(BF16)
    mine = lambda size, index: pl.ds(pl.multiple_of(index * size, size), size)
    ca = exchange(near["core"][1], lambda t: ga.at[mine(128, t)], ra1, *sems(tsem_a, 0))

    attn = attn_t.T.astype(BF16)
    skip = (xp.astype(F32) + nn(attn, w_out[...])).astype(BF16)
    skips[...] = skip
    cb = exchange(
        near["y"][1], lambda t: skips.at[mine(32, t // 2), mine(128, t % 2)], gx, tsem_b.at[0, :7], tsem_b.at[1, :7])

    d_normed_h = nt(d_kraw[OWN:], w_qkv[:, 256:512]) + nt(d_v[OWN:], w_qkv[:, 512:])
    hs[...] = d_normed_h.astype(BF16)
    ch = halo(1, reverse, [hs.at[s] for s in spans], [hr.at[s] for s in spans])
    wait_copies(ca)
    sa2[...] = (ga[mine(128, core)].astype(F32) + ra1[0].astype(F32)).astype(BF16)
    ca = exchange(near["x"][1], lambda t: sa2.at[mine(32, t)], ra2, *sems(tsem_a, 1))

    d_normed = (nt(d_q, w_qkv[:, :256]) + nt(d_kraw[:OWN], w_qkv[:, 256:512])) + nt(d_v[:OWN], w_qkv[:, 512:])
    gain_row = jnp.sum(xhat[:OWN] * d_normed, axis=0, keepdims=True) + jnp.sum(
        xh * inverse_h * d_normed_h, axis=0, keepdims=True)
    scale_row = jnp.sum(u * d_qhat, axis=0, keepdims=True)
    for i, r in enumerate((gain_row[:, :128], gain_row[:, 128:], scale_row[:, :128], scale_row[:, 128:])):
        g1[core, i : i + 1] = r
    g1[core, 4:8] = jnp.zeros((4, 128), F32)
    cg = spread(core, near["core"][1], g1, *sems(tsem_g, 0))

    unorder = one_hot(place_of(along(0, 128)), token_row)
    o_skip[...] = moved(unorder, skip)
    group = jnp.concatenate([skip[32 * g : 32 * g + 32] for g in range(4)], axis=1)
    o_merged[...] = nn(group, w_merge[...]).astype(BF16)
    saves[0].start()
    saves[1].start()
    wait_copies(cg)
    g2[x_at] = g1[0] + g1[1]
    cg = spread(x_at, near["x"][1], g2, *sems(tsem_g, 1))

    gx[7] = skips[mine(32, y_at // 2), mine(128, y_at % 2)]
    wait_copies(cd)
    wait_copies(cb)
    factor = nt(row_b[...], gx[...].reshape(256, 128)).astype(BF16)
    gb[...] = nn(factor, dmx[...].reshape(256, 512)).astype(BF16)
    cb = exchange(near["core"][1], lambda t: gb.at[mine(64, t)], rb1, tsem_b.at[0, 7:8], tsem_b.at[1, 7:8])

    wait_copies(ca)
    total = sa2[mine(32, x_at)].astype(F32)
    for p in range(3):
        total = total + ra2[p].astype(F32)
    total = jnp.concatenate(
        [jnp.concatenate([total[:, 192 * c : 192 * c + 192], total[:, 768 + 64 * c : 832 + 64 * c]], axis=1)
         for c in range(4)], axis=0)
    sa3[...] = moved(one_hot(slab_of(along(0, 128)), token_row), total.astype(BF16)).reshape(8, 16, 256)
    ca = exchange(near["y"][1], lambda t: sa3.at[t], ra3, *sems(tsem_a, 2))
    wait_copies(cg)
    g3[y_at] = (g2[0] + g2[1]) + (g2[2] + g2[3])
    cg = spread(y_at, near["y"][1], g3, *sems(tsem_g, 2))
    wait_copies(cb)
    sb2[...] = (gb[mine(64, core)].astype(F32) + rb1[0].astype(F32)).astype(BF16)
    cb = exchange(near["x"][1], lambda t: sb2.at[mine(16, t)], rb2, tsem_b.at[0, 8:11], tsem_b.at[1, 8:11])

    wait_copies(ch)
    d_normed = d_normed + nn(one_hot(token_of(along(0, 128)), sent_token(along(1, HALO))), hr[...])
    scaled = gains * d_normed
    x = xp.astype(F32)
    g_x = inverse * scaled - x * (inverse * inverse * inverse) * jnp.mean(x * scaled, axis=-1, keepdims=True)
    o_tokens[...] = moved(unorder, (keep[2] + g_x).astype(BF16))
    saves[2].start()

    wait_copies(cb)
    total = sb2[mine(16, x_at)].astype(F32)
    for p in range(3):
        total = total + rb2[p].astype(F32)
    sb4[...] = total
    cb = exchange(
        near["z"][1], lambda t: sb4.at[mine(8, t % 2), mine(128, t // 2)], rb4, tsem_b.at[0, 11:], tsem_b.at[1, 11:])

    wait_copies(ca)
    total = sa3[y_at].astype(F32)
    for p in range(7):
        total = total + ra3[p].astype(F32)
    sa4[...] = total.reshape(2, 8, 256)
    ca = exchange(near["z"][1], lambda t: sa4.at[t // 4], ra4, *sems(tsem_a, 3))
    wait_copies(cg)
    g4[z_at] = ((g3[0] + g3[1]) + (g3[2] + g3[3])) + ((g3[4] + g3[5]) + (g3[6] + g3[7]))
    cg = spread(z_at, near["z"][1], g4, *sems(tsem_g, 3))

    wait_copies(cb)
    total = sb4[mine(8, z_at % 2), mine(128, z_at // 2)]
    for p in range(7):
        total = total + rb4[p]
    o_merge[...] = total
    saves[5].start()
    wait_copies(ca)
    total = sa4[z_at // 4]
    for p in range(7):
        total = total + ra4[p]
    part = z_at % 4
    piece = jnp.zeros((2, 256), F32)
    for i in range(4):
        piece = piece + jnp.where(part == i, total[2 * i : 2 * i + 2], 0.0)
    o_qkv[...] = piece[:, :192]
    o_out[...] = piece[:, 192:]
    saves[3].start()
    saves[4].start()
    wait_copies(cg)
    total = ((g4[0] + g4[1]) + (g4[2] + g4[3])) + ((g4[4] + g4[5]) + (g4[6] + g4[7]))
    o_gain[...] = total[0:2]
    halves = lax.broadcasted_iota(jnp.int32, (1, 128), 1)
    out = jnp.zeros((1, 128), F32)
    for h in range(4):
        r = total[2 + h // 2 : 3 + h // 2]
        out = jnp.where(halves == h, jnp.sum(jnp.where(halves // 64 == h % 2, r, 0.0), axis=1, keepdims=True), out)
    o_scale[...] = out[:, :4]
    saves[6].start()
    saves[7].start()
    wait_copies(saves)


def hand_over(*refs):
    sources, targets, held, sem = refs[:8], refs[8:16], refs[16:24], refs[24]
    loads = start_copies([pltpu.make_async_copy(s, h, sem.at[0, i]) for i, (s, h) in enumerate(zip(sources, held))])
    saves = [pltpu.make_async_copy(h, t, sem.at[1, i]) for i, (h, t) in enumerate(zip(held, targets))]
    for load, save in zip(loads, saves):
        load.wait()
        save.start()
    wait_copies(saves)


def on_device(tokens, gain, w_qkv, head_scale, w_out, w_merge, d_merged, d_skip):
    V = pltpu.VMEM
    S = jax.ShapeDtypeStruct
    DMA = pltpu.SemaphoreType.DMA
    operands = (
        tokens.reshape(128, 256), gain.reshape(1, 256), w_qkv, head_scale.reshape(1, 4), w_out, w_merge,
        d_merged.reshape(32, 512), d_skip.reshape(128, 256),
    )
    results = (
        S((128, 256), BF16), S((32, 512), BF16), S((128, 256), BF16),
        S((2, 192), F32), S((2, 64), F32), S((8, 128), F32), S((2, 128), F32), S((1, 4), F32),
    )
    far = pl.BlockSpec(memory_space=pltpu.MemorySpace.HBM)
    out = pl.pallas_call(
        body,
        out_shape=results,
        in_specs=[far] * 8,
        out_specs=(far,) * 8,
        scratch_shapes=[V(a.shape, a.dtype) for a in operands + results] + [
            DMA((8,)), DMA((8,)),
            V((HALO, 256), BF16), V((96, 256), BF16), V((256, 256), BF16), V((128, 128), BF16), V((256, 256), BF16),
            V((NK, 512), BF16), V((512, NK), BF16),
            V((NK, 512), F32), V((NK, 512), F32), V((NK, 512), BF16), V((NK, 512), BF16),
            V((512, 256), BF16), V((512, 256), BF16), V((3, 128, 256), F32), V((2, NK, 256), F32), V((OWN, 256), F32),
            V((256, NK), BF16), V((HALO, 256), BF16), V((HALO, 256), BF16), V((NK, 128), F32),
            V((256, 1024), BF16), V((1, 128, 1024), BF16),
            V((128, 1024), BF16), V((3, 32, 1024), BF16),
            V((8, 16, 256), BF16), V((7, 16, 256), BF16),
            V((2, 8, 256), F32), V((7, 8, 256), F32),
            V((128, 256), BF16), V((8, 32, 128), BF16), V((8, 32, 512), BF16),
            V((128, 512), BF16), V((1, 64, 512), BF16),
            V((64, 512), BF16), V((3, 16, 512), BF16),
            V((16, 512), F32), V((7, 8, 128), F32),
            V((2, 8, 128), F32), V((4, 8, 128), F32), V((8, 8, 128), F32), V((8, 8, 128), F32),
            DMA((2, 28)), DMA((2, 18)), DMA((2, 7)), DMA((2, 28)), DMA((2, 16)),
        ],
        compiler_params=pltpu.CompilerParams(collective_id=0, has_side_effects=True, vmem_limit_bytes=VMEM_LIMIT),
    )(*operands)
    out = pl.pallas_call(
        hand_over,
        out_shape=results,
        in_specs=[far] * 8,
        out_specs=(far,) * 8,
        scratch_shapes=[V(a.shape, a.dtype) for a in results] + [DMA((2, 8))],
        compiler_params=pltpu.CompilerParams(vmem_limit_bytes=VMEM_LIMIT),
    )(*out)
    skip, merged, grad, qkv, o, m, g, s = out
    return (skip.reshape(4, 32, 256), merged.reshape(2, 16, 512), grad.reshape(4, 32, 256), qkv, o, m, g.reshape(256), s.reshape(4))


def solution(mesh):
    return jax.shard_map(
        on_device,
        mesh=mesh,
        in_specs=(
            P("row", "col", None),
            P(),
            P(),
            P(),
            P(),
            P(),
            P("row", "col", None),
            P("row", "col", None),
        ),
        out_specs=(
            P("row", "col", None),
            P("row", "col", None),
            P("row", "col", None),
            P("row", "col"),
            P("row", "col"),
            P("row", "col"),
            P(),
            P(),
        ),
        check_vma=False,
    )
```

```python
import jax
import jax.numpy as jnp
from jax import lax
from jax.experimental import pallas as pl
from jax.experimental.pallas import tpu as pltpu
from jax.sharding import PartitionSpec as P

EPS = 1e-06
MESH = pl.DeviceIdType.MESH
NX, NY, NZ = 4, 8, 8
ROWS, COLS = 128, 4
F32, BF16 = jnp.float32, jnp.bfloat16
OWN, NK = 128, 416
VMEM_LIMIT = 63 * 2**20
HALO = NK - OWN


def place():
    row, col = lax.axis_index("row"), lax.axis_index("col")
    return row >> 4, (row >> 3) & 1, (row >> 1) & 3, row & 1, col


def device(y, zl, x, core, col):
    return ((y << 4) | (zl << 3) | (x << 1) | core, col)


def peers():
    y, zl, x, core, col = place()
    z = col * 2 + zl
    out = {"core": (core, [(1 - core, device(y, zl, x, 1 - core, col))])}
    out["x"] = (x, [])
    for p in range(1, NX):
        t = (x + p) & (NX - 1)
        out["x"][1].append((t, device(y, zl, t, core, col)))
    out["y"] = (y, [])
    for p in range(1, NY):
        t = (y + p) & (NY - 1)
        out["y"][1].append((t, device(t, zl, x, core, col)))
    out["z"] = (z, [])
    for p in range(1, NZ):
        t = (z + p) & (NZ - 1)
        out["z"][1].append((t, device(y, t & 1, x, core, t >> 1)))
    return out


def start_copies(copies):
    for c in copies:
        c.start()
    return copies


def wait_copies(copies):
    for c in copies:
        c.wait()


def arrived(copies, sent):
    for c in copies:
        c.wait_recv()
    sent.extend(copies)


def drain(sent):
    for c in sent:
        c.wait_send()
    sent.clear()


def exchange(peer_list, source, slots, send, recv):
    return start_copies(
        [
            pltpu.make_async_remote_copy(
                src_ref=source(t),
                dst_ref=slots.at[p],
                send_sem=send.at[p],
                recv_sem=recv.at[p],
                device_id=dev,
                device_id_type=MESH,
            )
            for p, (t, dev) in enumerate(peer_list)
        ]
    )


def spread(mine, peer_list, slots, send, recv):
    return start_copies(
        [
            pltpu.make_async_remote_copy(
                src_ref=slots.at[mine],
                dst_ref=slots.at[mine],
                send_sem=send.at[p],
                recv_sem=recv.at[p],
                device_id=dev,
                device_id_type=MESH,
            )
            for p, (t, dev) in enumerate(peer_list)
        ]
    )


def along(axis, size):
    return lax.broadcasted_iota(jnp.int32, (size, 1) if axis == 0 else (1, size), axis)


def token_of(p):
    return ((((p >> 4) & 1) * 2 + (p >> 6)) << 5) + (p & 15) * 2 + ((p >> 5) & 1)


def place_of(t):
    r, c = t >> 5, t & 31
    return ((r & 1) * 2 + (c & 1)) * 32 + (r >> 1) * 16 + (c >> 1)


def third(k):
    return (k * 11) >> 5


def slot_token(i):
    s, k = i >> 4, i & 15
    r = third(k) + jnp.where((s == 2) | (s == 3), 1, 0)
    c = k - 3 * third(k) + jnp.where((s & 1) == 0, 29, 0)
    return jnp.where(k < jnp.where(s < 2, 12, 9), r * 32 + c, -1)


def sent_token(k):
    return jnp.where(k < 96, k + 32, jnp.where(k < 192, k - 96, slot_token(k - 192)))


def row_a_of(n):
    return ((((n >> 2) & 7) * 2 + ((n >> 1) & 1)) * 4 + ((n >> 5) & 3)) * 4 + (n >> 7) * 2 + (n & 1)


def row_b_of(n):
    return ((n >> 3) & 1) * 64 + ((n >> 4) & 3) * 16 + (n >> 6) * 8 + (n & 7)


def slab_of(n):
    return ((n >> 2) & 3) * 32 + (n >> 4) * 4 + (n & 3)


def one_hot(rows, cols):
    return jnp.where(rows == cols, 1.0, 0.0).astype(BF16)


def allowed_keys(row, col):
    n, p = along(0, NK), along(1, 128)
    own = token_of(n)
    i = n - 320
    s, k = i >> 4, i & 15
    slot_r = third(k) + jnp.where(s < 2, 0, jnp.where(s < 4, -3, 4))
    slot_c = k - 3 * third(k) + jnp.where((s & 1) == 0, -3, 32)
    slot_r = jnp.where(k < jnp.where(s < 2, 12, 9), slot_r, 1000)
    side = jnp.where(n < 224, n - 128, n - 224)
    kr = jnp.where(n < 128, own >> 5, jnp.where(n < 320, (side >> 5) + jnp.where(n < 224, -3, 4), slot_r))
    kc = jnp.where(n < 128, own & 31, jnp.where(n < 320, side & 31, slot_c))
    inside = (kr + 4 * row >= 0) & (kr + 4 * row < 4 * ROWS) & (kc + 32 * col >= 0) & (kc + 32 * col < 32 * COLS)
    kr = jnp.where(inside, kr, 1000)
    query = token_of(p)
    return jnp.where((jnp.abs(kr - (query >> 5)) <= 3) & (jnp.abs(kc - (query & 31)) <= 3), 1.0, 0.0)


def nt(a, b):
    return lax.dot_general(a, b, (((1,), (1,)), ((), ())), preferred_element_type=F32)


def nn(a, b):
    return jnp.dot(a, b, preferred_element_type=F32)


def moved(table, value):
    return nn(table, value).astype(BF16)


def head_sums(value, ones):
    big = value.astype(BF16)
    small = (value - big.astype(F32)).astype(BF16)
    return nn(big, ones) + nn(small, ones)


def norm_rows(x, gain):
    inverse = lax.rsqrt(jnp.mean(x * x, axis=-1, keepdims=True) + EPS)
    return inverse, (x * inverse * gain).astype(BF16)


def body(*refs):
    sources, targets, held, ready, (load_sem, save_sem), work = (
        refs[:8], refs[8:16], refs[16:24], refs[24:32], refs[32:34], refs[34:])
    loads = [pltpu.make_async_copy(s, t, load_sem.at[i]) for i, (s, t) in enumerate(zip(sources, held))]
    saves = [pltpu.make_async_copy(s, t, save_sem.at[i]) for i, (s, t) in enumerate(zip(ready, targets))]
    compute(loads, saves, *held, *ready, *work)


FIRST = (0, 2, 1, 3, 6, 7, 5, 4)


def compute(loads, saves, tokens, gain, w_qkv, head_scale, w_out, w_merge, d_merged, d_skip,
         o_skip, o_merged, o_tokens, o_qkv, o_out, o_merge, o_gain, o_scale,
         xk, strips, row_a, row_b, ones_t, kv, kvt, st, pt, ptb, dst, q4, da4, keep, keys, xhat, nt_all, hs, hr, allowed,
         ga, ra1, sa2, ra2, sa3, ra3, sa4, ra4,
         skips, gx, dmx, gb, rb1, sb2, rb2, sb4, rb4,
         g1, g2, g3, g4, tsem_a, tsem_b, tsem_d, tsem_g, tsem_h):
    near = peers()
    sent = []
    core, x_at, y_at, z_at = (near[a][0] for a in ("core", "x", "y", "z"))
    row, col = lax.axis_index("row"), lax.axis_index("col")
    up, down = (row + ROWS - 1) & (ROWS - 1), (row + 1) & (ROWS - 1)
    left, right = (col + COLS - 1) & (COLS - 1), (col + 1) & (COLS - 1)
    toward = [(down, col), (up, col), (row, right), (row, left), (down, right), (down, left), (up, right), (up, left)]
    reverse = [(up, col), (down, col), (row, left), (row, right), (up, left), (up, right), (down, left), (down, right)]
    bar = pltpu.get_barrier_semaphore()
    for dev in toward[4:] + toward[:4]:
        pl.semaphore_signal(bar, inc=1, device_id=dev, device_id_type=MESH)
    for i in FIRST:
        loads[i].start()
    for axis in ("core", "x", "y", "z"):
        for _, dev in near[axis][1]:
            pl.semaphore_signal(bar, inc=1, device_id=dev, device_id_type=MESH)

    def sems(table, stage):
        return table.at[0, pl.ds(7 * stage, 7)], table.at[1, pl.ds(7 * stage, 7)]

    def halo(stage, devices, sources, targets):
        return start_copies([
            pltpu.make_async_remote_copy(
                src_ref=s, dst_ref=t, send_sem=tsem_h.at[0, 8 * stage + i], recv_sem=tsem_h.at[1, 8 * stage + i],
                device_id=dev, device_id_type=MESH)
            for i, (dev, s, t) in reversed(list(enumerate(zip(devices, sources, targets))))
        ])

    def loaded(*names):
        for i in names:
            loads[i].wait()

    token_row = along(1, 128)
    pick = one_hot(slot_token(along(0, 96)), token_row)
    loaded(0)
    strips[...] = moved(pick, tokens[...])
    pl.semaphore_wait(bar, 8 + 1 + 3 + 7 + 7)
    spans = [pl.ds(0, 96), pl.ds(96, 96)] + [pl.ds(192 + 16 * s, 16) for s in range(6)]
    ch = halo(
        0, toward,
        [tokens.at[pl.ds(32, 96)], tokens.at[pl.ds(0, 96)]] + [strips.at[pl.ds(16 * s, 16)] for s in range(6)],
        [xk.at[s] for s in spans],
    )


    loaded(6)
    dmx[7] = d_merged[...]
    cd = exchange(near["y"][1], lambda t: d_merged, dmx, tsem_d.at[0], tsem_d.at[1])

    order = one_hot(token_of(along(0, 128)), token_row)
    feature = along(1, 256)
    row_a[...] = one_hot(row_a_of(along(0, 256)), feature)
    row_b[...] = one_hot(row_b_of(along(0, 128)), token_row)
    ones_t[...] = one_hot(along(0, 256) >> 6, feature >> 6)
    allowed[...] = allowed_keys(row, col)

    loaded(1, 2, 3)
    ones = ones_t[...]
    gains = gain[...]
    lane = lax.broadcasted_iota(jnp.int32, (1, 256), 1) // 64
    scales = jnp.zeros((1, 256), F32)
    for h in range(4):
        scales = jnp.where(lane == h, head_scale[:, h : h + 1], scales)
    xp = moved(order, tokens[...])
    x = xp.astype(F32)
    inverse, normed = norm_rows(x, gains)
    xhat[:OWN] = x * inverse
    nt_all[:, :OWN] = nt(row_a[...], normed).astype(BF16)
    qkv = nn(normed, w_qkv[...])
    q, k = qkv[:, :256], qkv[:, 256:512]
    q_norm = lax.rsqrt(head_sums(q * q, ones) + EPS)
    k_norm = lax.rsqrt(head_sums(k * k, ones) + EPS)
    q_unit, k_unit = q * q_norm, k * k_norm
    q_hat = (q_unit * scales).astype(BF16)
    keep[0], keep[1] = q_norm, q_unit
    keys[0, :OWN], keys[1, :OWN] = k_norm, k_unit
    kv[:OWN, :256] = k_unit.astype(BF16)
    kv[:OWN, 256:] = qkv[:, 512:].astype(BF16)
    zero = jnp.zeros((), BF16)
    for h in range(4):
        q4[128 * h : 128 * h + 128] = jnp.where(lane == h, q_hat, zero)

    loaded(4, 5, 7)
    d_group = nt(d_merged[...], w_merge[...])
    d_y = moved(order, d_skip[...]).astype(F32) + jnp.concatenate(
        [d_group[:, 256 * g : 256 * g + 256] for g in range(4)], axis=0)
    dy_b = d_y.astype(BF16)
    keep[2] = d_y
    d_attn = nt(dy_b, w_out[...]).astype(BF16)
    for h in range(4):
        da4[128 * h : 128 * h + 128] = jnp.where(lane == h, d_attn, zero)


    arrived(ch, sent)
    xh = xk[...].astype(F32)
    inverse_h, normed_h = norm_rows(xh, gains)
    kv_h = nn(normed_h, w_qkv[:, 256:])
    k_h = kv_h[:, :256]
    k_norm_h = lax.rsqrt(head_sums(k_h * k_h, ones) + EPS)
    k_unit_h = k_h * k_norm_h
    keys[0, OWN:], keys[1, OWN:] = k_norm_h, k_unit_h
    kv[OWN:, :256] = k_unit_h.astype(BF16)
    kv[OWN:, 256:] = kv_h[:, 256:].astype(BF16)

    st[...] = nt(kv[:, :256], q4[...])
    for h in range(4):
        span = slice(128 * h, 128 * h + 128)
        e = jnp.exp(st[:, span]) * allowed[...]
        p = e * (1.0 / jnp.sum(e, axis=0, keepdims=True))
        pt[:, span] = p
        ptb[:, span] = p.astype(BF16)

    st[...] = nt(kv[:, 256:], da4[...])
    for h in range(4):
        span = slice(128 * h, 128 * h + 128)
        dw, p = st[:, span], pt[:, span]
        dst[:, span] = (p * (dw - jnp.sum(dw * p, axis=0, keepdims=True))).astype(BF16)
    d_k = nn(dst[...], q4[...])
    ku = keys[1]
    d_kraw = (keys[0] * (d_k - ku * head_sums(ku * d_k, ones))).astype(BF16)
    d_v = nn(ptb[...], da4[...]).astype(BF16)
    nt_all[:, OWN:] = nt(row_a[...], normed_h).astype(BF16)
    normed_t = nt_all[...]
    eye = one_hot(along(0, 256), feature)
    kvt[:256] = nt(eye, kv[:, :256]).astype(BF16)
    kvt[256:] = nt(eye, kv[:, 256:]).astype(BF16)

    def diagonal(full):
        return jnp.concatenate([full[64 * h : 64 * h + 64, 128 * h : 128 * h + 128] for h in range(4)], axis=0)

    d_qhat = diagonal(nn(kvt[:256], dst[...])).T
    u = keep[1]
    g_u = d_qhat * scales
    d_q = (keep[0] * (g_u - u * head_sums(u * g_u, ones))).astype(BF16)
    attn_t = diagonal(nn(kvt[256:], ptb[...]))
    ga[:, :256] = nn(normed_t[:, :OWN], d_q).astype(BF16)
    ga[:, 256:512] = nn(normed_t, d_kraw).astype(BF16)
    ga[:, 512:768] = nn(normed_t, d_v).astype(BF16)
    ga[:, 768:] = nn(nn(row_a[...], attn_t.astype(BF16)).astype(BF16), keep[2].astype(BF16)).astype(BF16)
    mine = lambda size, index: pl.ds(pl.multiple_of(index * size, size), size)
    ca = exchange(near["core"][1], lambda t: ga.at[mine(128, t)], ra1, *sems(tsem_a, 0))

    attn = attn_t.T.astype(BF16)
    skip = (xp.astype(F32) + nn(attn, w_out[...])).astype(BF16)
    skips[...] = skip
    cb = exchange(
        near["y"][1], lambda t: skips.at[mine(32, t >> 1), mine(128, t & 1)], gx, tsem_b.at[0, :7], tsem_b.at[1, :7])

    d_normed_h = nt(d_kraw[OWN:], w_qkv[:, 256:512]) + nt(d_v[OWN:], w_qkv[:, 512:])
    hs[...] = d_normed_h.astype(BF16)
    arrived(ca, sent)
    sa2[...] = (ga[mine(128, core)].astype(F32) + ra1[0].astype(F32)).astype(BF16)
    ca = exchange(near["x"][1], lambda t: sa2.at[mine(32, t)], ra2, *sems(tsem_a, 1))
    ch = halo(1, reverse, [hs.at[s] for s in spans], [hr.at[s] for s in spans])

    d_normed = (nt(d_q, w_qkv[:, :256]) + nt(d_kraw[:OWN], w_qkv[:, 256:512])) + nt(d_v[:OWN], w_qkv[:, 512:])
    gain_row = jnp.sum(xhat[:OWN] * d_normed, axis=0, keepdims=True) + jnp.sum(
        xh * inverse_h * d_normed_h, axis=0, keepdims=True)
    scale_row = jnp.sum(u * d_qhat, axis=0, keepdims=True)
    for i, r in enumerate((gain_row[:, :128], gain_row[:, 128:], scale_row[:, :128], scale_row[:, 128:])):
        g1[core, i : i + 1] = r
    g1[core, 4:8] = jnp.zeros((4, 128), F32)
    cg = spread(core, near["core"][1], g1, *sems(tsem_g, 0))

    unorder = one_hot(place_of(along(0, 128)), token_row)
    o_skip[...] = moved(unorder, skip)
    group = jnp.concatenate([skip[32 * g : 32 * g + 32] for g in range(4)], axis=1)
    o_merged[...] = nn(group, w_merge[...]).astype(BF16)
    saves[0].start()
    saves[1].start()
    arrived(cg, sent)
    g2[x_at] = g1[0] + g1[1]
    cg = spread(x_at, near["x"][1], g2, *sems(tsem_g, 1))

    gx[7] = skips[mine(32, y_at >> 1), mine(128, y_at & 1)]
    arrived(cd, sent)
    arrived(cb, sent)
    factor = nt(row_b[...], gx[...].reshape(256, 128)).astype(BF16)
    gb[...] = nn(factor, dmx[...].reshape(256, 512)).astype(BF16)
    cb = exchange(near["core"][1], lambda t: gb.at[mine(64, t)], rb1, tsem_b.at[0, 7:8], tsem_b.at[1, 7:8])

    arrived(ca, sent)
    total = sa2[mine(32, x_at)].astype(F32)
    for p in range(3):
        total = total + ra2[p].astype(F32)
    total = jnp.concatenate(
        [jnp.concatenate([total[:, 192 * c : 192 * c + 192], total[:, 768 + 64 * c : 832 + 64 * c]], axis=1)
         for c in range(4)], axis=0)
    sa3[...] = moved(one_hot(slab_of(along(0, 128)), token_row), total.astype(BF16)).reshape(8, 16, 256)
    ca = exchange(near["y"][1], lambda t: sa3.at[t], ra3, *sems(tsem_a, 2))
    arrived(cg, sent)
    g3[y_at] = (g2[0] + g2[1]) + (g2[2] + g2[3])
    cg = spread(y_at, near["y"][1], g3, *sems(tsem_g, 2))
    arrived(cb, sent)
    sb2[...] = (gb[mine(64, core)].astype(F32) + rb1[0].astype(F32)).astype(BF16)
    cb = exchange(near["x"][1], lambda t: sb2.at[mine(16, t)], rb2, tsem_b.at[0, 8:11], tsem_b.at[1, 8:11])

    arrived(ch, sent)
    d_normed = d_normed + nn(one_hot(token_of(along(0, 128)), sent_token(along(1, HALO))), hr[...])
    scaled = gains * d_normed
    x = xp.astype(F32)
    g_x = inverse * scaled - x * (inverse * inverse * inverse) * jnp.mean(x * scaled, axis=-1, keepdims=True)
    o_tokens[...] = moved(unorder, (keep[2] + g_x).astype(BF16))
    saves[2].start()

    arrived(cb, sent)
    total = sb2[mine(16, x_at)].astype(F32)
    for p in range(3):
        total = total + rb2[p].astype(F32)
    sb4[...] = total
    cb = exchange(
        near["z"][1], lambda t: sb4.at[mine(8, t & 1), mine(128, t >> 1)], rb4, tsem_b.at[0, 11:], tsem_b.at[1, 11:])

    arrived(ca, sent)
    total = sa3[y_at].astype(F32)
    for p in range(7):
        total = total + ra3[p].astype(F32)
    sa4[...] = total.reshape(2, 8, 256)
    ca = exchange(near["z"][1], lambda t: sa4.at[t >> 2], ra4, *sems(tsem_a, 3))
    arrived(cg, sent)
    g4[z_at] = ((g3[0] + g3[1]) + (g3[2] + g3[3])) + ((g3[4] + g3[5]) + (g3[6] + g3[7]))
    cg = spread(z_at, near["z"][1], g4, *sems(tsem_g, 3))

    drain(sent)
    for c in ca + cb + cg:
        c.wait_send()
    last = []
    arrived(cb, last)
    total = sb4[mine(8, z_at & 1), mine(128, z_at >> 1)]
    for p in range(7):
        total = total + rb4[p]
    o_merge[...] = total
    saves[5].start()
    arrived(ca, last)
    total = sa4[z_at >> 2]
    for p in range(7):
        total = total + ra4[p]
    part = z_at & 3
    piece = jnp.zeros((2, 256), F32)
    for i in range(4):
        piece = piece + jnp.where(part == i, total[2 * i : 2 * i + 2], 0.0)
    o_qkv[...] = piece[:, :192]
    o_out[...] = piece[:, 192:]
    saves[3].start()
    saves[4].start()
    arrived(cg, last)
    total = ((g4[0] + g4[1]) + (g4[2] + g4[3])) + ((g4[4] + g4[5]) + (g4[6] + g4[7]))
    o_gain[...] = total[0:2]
    halves = lax.broadcasted_iota(jnp.int32, (1, 128), 1)
    out = jnp.zeros((1, 128), F32)
    for h in range(4):
        r = total[2 + h // 2 : 3 + h // 2]
        out = jnp.where(halves == h, jnp.sum(jnp.where(halves // 64 == h % 2, r, 0.0), axis=1, keepdims=True), out)
    o_scale[...] = out[:, :4]
    saves[6].start()
    saves[7].start()
    wait_copies(saves)


def hand_over(*refs):
    sources, targets, held, sem = refs[:8], refs[8:16], refs[16:24], refs[24]
    loads = start_copies([pltpu.make_async_copy(s, h, sem.at[0, i]) for i, (s, h) in enumerate(zip(sources, held))])
    saves = [pltpu.make_async_copy(h, t, sem.at[1, i]) for i, (h, t) in enumerate(zip(held, targets))]
    for load, save in zip(loads, saves):
        load.wait()
        save.start()
    wait_copies(saves)


def on_device(tokens, gain, w_qkv, head_scale, w_out, w_merge, d_merged, d_skip):
    V = pltpu.VMEM
    S = jax.ShapeDtypeStruct
    DMA = pltpu.SemaphoreType.DMA
    operands = (
        tokens.reshape(128, 256), gain.reshape(1, 256), w_qkv, head_scale.reshape(1, 4), w_out, w_merge,
        d_merged.reshape(32, 512), d_skip.reshape(128, 256),
    )
    results = (
        S((128, 256), BF16), S((32, 512), BF16), S((128, 256), BF16),
        S((2, 192), F32), S((2, 64), F32), S((8, 128), F32), S((2, 128), F32), S((1, 4), F32),
    )
    far = pl.BlockSpec(memory_space=pltpu.MemorySpace.HBM)
    out = pl.pallas_call(
        body,
        out_shape=results,
        in_specs=[far] * 8,
        out_specs=(far,) * 8,
        scratch_shapes=[V(a.shape, a.dtype) for a in operands + results] + [
            DMA((8,)), DMA((8,)),
            V((HALO, 256), BF16), V((96, 256), BF16), V((256, 256), BF16), V((128, 128), BF16), V((256, 256), BF16),
            V((NK, 512), BF16), V((512, NK), BF16),
            V((NK, 512), F32), V((NK, 512), F32), V((NK, 512), BF16), V((NK, 512), BF16),
            V((512, 256), BF16), V((512, 256), BF16), V((3, 128, 256), F32), V((2, NK, 256), F32), V((OWN, 256), F32),
            V((256, NK), BF16), V((HALO, 256), BF16), V((HALO, 256), BF16), V((NK, 128), F32),
            V((256, 1024), BF16), V((1, 128, 1024), BF16),
            V((128, 1024), BF16), V((3, 32, 1024), BF16),
            V((8, 16, 256), BF16), V((7, 16, 256), BF16),
            V((2, 8, 256), F32), V((7, 8, 256), F32),
            V((128, 256), BF16), V((8, 32, 128), BF16), V((8, 32, 512), BF16),
            V((128, 512), BF16), V((1, 64, 512), BF16),
            V((64, 512), BF16), V((3, 16, 512), BF16),
            V((16, 512), F32), V((7, 8, 128), F32),
            V((2, 8, 128), F32), V((4, 8, 128), F32), V((8, 8, 128), F32), V((8, 8, 128), F32),
            DMA((2, 28)), DMA((2, 18)), DMA((2, 7)), DMA((2, 28)), DMA((2, 16)),
        ],
        compiler_params=pltpu.CompilerParams(collective_id=0, has_side_effects=True, vmem_limit_bytes=VMEM_LIMIT),
    )(*operands)
    out = pl.pallas_call(
        hand_over,
        out_shape=results,
        in_specs=[far] * 8,
        out_specs=(far,) * 8,
        scratch_shapes=[V(a.shape, a.dtype) for a in results] + [DMA((2, 8))],
        compiler_params=pltpu.CompilerParams(vmem_limit_bytes=VMEM_LIMIT),
    )(*out)
    skip, merged, grad, qkv, o, m, g, s = out
    return (skip.reshape(4, 32, 256), merged.reshape(2, 16, 512), grad.reshape(4, 32, 256), qkv, o, m, g.reshape(256), s.reshape(4))


def solution(mesh):
    return jax.shard_map(
        on_device,
        mesh=mesh,
        in_specs=(
            P("row", "col", None),
            P(),
            P(),
            P(),
            P(),
            P(),
            P("row", "col", None),
            P("row", "col", None),
        ),
        out_specs=(
            P("row", "col", None),
            P("row", "col", None),
            P("row", "col", None),
            P("row", "col"),
            P("row", "col"),
            P("row", "col"),
            P(),
            P(),
        ),
        check_vma=False,
    )
```

```python
import jax
import jax.numpy as jnp
from jax import lax
from jax.experimental import pallas as pl
from jax.experimental.pallas import tpu as pltpu
from jax.sharding import PartitionSpec as P

EPS = 1e-06
MESH = pl.DeviceIdType.MESH
NX, NY, NZ = 4, 8, 8
ROWS, COLS = 128, 4
F32, BF16 = jnp.float32, jnp.bfloat16
OWN, NK = 128, 416
VMEM_LIMIT = 63 * 2**20
HALO = NK - OWN


def place():
    row, col = lax.axis_index("row"), lax.axis_index("col")
    return row >> 4, (row >> 3) & 1, (row >> 1) & 3, row & 1, col


def device(y, zl, x, core, col):
    return ((y << 4) | (zl << 3) | (x << 1) | core, col)


def peers():
    y, zl, x, core, col = place()
    z = col * 2 + zl
    out = {"core": (core, [(1 - core, device(y, zl, x, 1 - core, col))])}
    out["x"] = (x, [])
    for p in range(1, NX):
        t = (x + p) & (NX - 1)
        out["x"][1].append((t, device(y, zl, t, core, col)))
    out["y"] = (y, [])
    for p in range(1, NY):
        t = (y + p) & (NY - 1)
        out["y"][1].append((t, device(t, zl, x, core, col)))
    out["z"] = (z, [])
    for p in range(1, NZ):
        t = (z + p) & (NZ - 1)
        out["z"][1].append((t, device(y, t & 1, x, core, t >> 1)))
    return out


def start_copies(copies):
    for c in copies:
        c.start()
    return copies


def wait_copies(copies):
    for c in copies:
        c.wait()


def arrived(copies, sent):
    for c in copies:
        c.wait_recv()
    sent.extend(copies)


def drain(sent):
    for c in sent:
        c.wait_send()
    sent.clear()


def exchange(peer_list, source, slots, send, recv):
    return start_copies(
        [
            pltpu.make_async_remote_copy(
                src_ref=source(t),
                dst_ref=slots.at[p],
                send_sem=send.at[p],
                recv_sem=recv.at[p],
                device_id=dev,
                device_id_type=MESH,
            )
            for p, (t, dev) in enumerate(peer_list)
        ]
    )


def spread(mine, peer_list, slots, send, recv):
    return start_copies(
        [
            pltpu.make_async_remote_copy(
                src_ref=slots.at[mine],
                dst_ref=slots.at[mine],
                send_sem=send.at[p],
                recv_sem=recv.at[p],
                device_id=dev,
                device_id_type=MESH,
            )
            for p, (t, dev) in enumerate(peer_list)
        ]
    )


def along(axis, size):
    return lax.broadcasted_iota(jnp.int32, (size, 1) if axis == 0 else (1, size), axis)


def token_of(p):
    return ((((p >> 4) & 1) * 2 + (p >> 6)) << 5) + (p & 15) * 2 + ((p >> 5) & 1)


def place_of(t):
    r, c = t >> 5, t & 31
    return ((r & 1) * 2 + (c & 1)) * 32 + (r >> 1) * 16 + (c >> 1)


def third(k):
    return (k * 11) >> 5


def slot_token(i):
    s, k = i >> 4, i & 15
    r = third(k) + jnp.where((s == 2) | (s == 3), 1, 0)
    c = k - 3 * third(k) + jnp.where((s & 1) == 0, 29, 0)
    return jnp.where(k < jnp.where(s < 2, 12, 9), r * 32 + c, -1)


def sent_token(k):
    return jnp.where(k < 96, k + 32, jnp.where(k < 192, k - 96, slot_token(k - 192)))


def row_a_of(n):
    return ((((n >> 2) & 7) * 2 + ((n >> 1) & 1)) * 4 + ((n >> 5) & 3)) * 4 + (n >> 7) * 2 + (n & 1)


def row_b_of(n):
    return ((n >> 3) & 1) * 64 + ((n >> 4) & 3) * 16 + (n >> 6) * 8 + (n & 7)


def slab_of(n):
    return ((n >> 2) & 3) * 32 + (n >> 4) * 4 + (n & 3)


def one_hot(rows, cols):
    return jnp.where(rows == cols, 1.0, 0.0).astype(BF16)


def allowed_keys(row, col):
    n, p = along(0, NK), along(1, 128)
    own = token_of(n)
    i = n - 320
    s, k = i >> 4, i & 15
    slot_r = third(k) + jnp.where(s < 2, 0, jnp.where(s < 4, -3, 4))
    slot_c = k - 3 * third(k) + jnp.where((s & 1) == 0, -3, 32)
    slot_r = jnp.where(k < jnp.where(s < 2, 12, 9), slot_r, 1000)
    side = jnp.where(n < 224, n - 128, n - 224)
    kr = jnp.where(n < 128, own >> 5, jnp.where(n < 320, (side >> 5) + jnp.where(n < 224, -3, 4), slot_r))
    kc = jnp.where(n < 128, own & 31, jnp.where(n < 320, side & 31, slot_c))
    inside = (kr + 4 * row >= 0) & (kr + 4 * row < 4 * ROWS) & (kc + 32 * col >= 0) & (kc + 32 * col < 32 * COLS)
    kr = jnp.where(inside, kr, 1000)
    query = token_of(p)
    return jnp.where((jnp.abs(kr - (query >> 5)) <= 3) & (jnp.abs(kc - (query & 31)) <= 3), 1.0, 0.0)


def nt(a, b):
    return lax.dot_general(a, b, (((1,), (1,)), ((), ())), preferred_element_type=F32)


def nn(a, b):
    return jnp.dot(a, b, preferred_element_type=F32)


def moved(table, value):
    return nn(table, value).astype(BF16)


def head_sums(value, ones):
    big = value.astype(BF16)
    small = (value - big.astype(F32)).astype(BF16)
    return nn(big, ones) + nn(small, ones)


def norm_rows(x, gain):
    inverse = lax.rsqrt(jnp.mean(x * x, axis=-1, keepdims=True) + EPS)
    return inverse, (x * inverse * gain).astype(BF16)


def body(*refs):
    sources, targets, held, ready, (load_sem, save_sem), work = (
        refs[:8], refs[8:16], refs[16:24], refs[24:32], refs[32:34], refs[34:])
    loads = [pltpu.make_async_copy(s, t, load_sem.at[i]) for i, (s, t) in enumerate(zip(sources, held))]
    saves = [pltpu.make_async_copy(s, t, save_sem.at[i]) for i, (s, t) in enumerate(zip(ready, targets))]
    compute(loads, saves, *held, *ready, *work)


FIRST = (0, 2, 1, 3, 6, 7, 5, 4)


def compute(loads, saves, tokens, gain, w_qkv, head_scale, w_out, w_merge, d_merged, d_skip,
         o_skip, o_merged, o_tokens, o_qkv, o_out, o_merge, o_gain, o_scale,
         xk, strips, row_a, row_b, ones_t, kv, kvt, st, dwt, ptb, dst, q4, da4, keep, keys, xhat, nt_all, hs, hr, allowed,
         ga, ra1, sa2, ra2, sa3, ra3, sa4, ra4,
         skips, gx, dmx, gb, rb1, sb2, rb2, sb4, rb4,
         g1, g2, g3, g4, tsem_a, tsem_b, tsem_d, tsem_g, tsem_h):
    near = peers()
    sent = []
    core, x_at, y_at, z_at = (near[a][0] for a in ("core", "x", "y", "z"))
    row, col = lax.axis_index("row"), lax.axis_index("col")
    up, down = (row + ROWS - 1) & (ROWS - 1), (row + 1) & (ROWS - 1)
    left, right = (col + COLS - 1) & (COLS - 1), (col + 1) & (COLS - 1)
    toward = [(down, col), (up, col), (row, right), (row, left), (down, right), (down, left), (up, right), (up, left)]
    reverse = [(up, col), (down, col), (row, left), (row, right), (up, left), (up, right), (down, left), (down, right)]
    bar = pltpu.get_barrier_semaphore()
    for dev in toward[4:] + toward[:4]:
        pl.semaphore_signal(bar, inc=1, device_id=dev, device_id_type=MESH)
    for i in FIRST:
        loads[i].start()
    for axis in ("core", "x", "y", "z"):
        for _, dev in near[axis][1]:
            pl.semaphore_signal(bar, inc=1, device_id=dev, device_id_type=MESH)

    def sems(table, stage):
        return table.at[0, pl.ds(7 * stage, 7)], table.at[1, pl.ds(7 * stage, 7)]

    def halo(stage, devices, sources, targets):
        return start_copies([
            pltpu.make_async_remote_copy(
                src_ref=s, dst_ref=t, send_sem=tsem_h.at[0, 8 * stage + i], recv_sem=tsem_h.at[1, 8 * stage + i],
                device_id=dev, device_id_type=MESH)
            for i, (dev, s, t) in reversed(list(enumerate(zip(devices, sources, targets))))
        ])

    def loaded(*names):
        for i in names:
            loads[i].wait()

    token_row = along(1, 128)
    pick = one_hot(slot_token(along(0, 96)), token_row)
    loaded(0)
    strips[...] = moved(pick, tokens[...])
    pl.semaphore_wait(bar, 8 + 1 + 3 + 7 + 7)
    spans = [pl.ds(0, 96), pl.ds(96, 96)] + [pl.ds(192 + 16 * s, 16) for s in range(6)]
    ch = halo(
        0, toward,
        [tokens.at[pl.ds(32, 96)], tokens.at[pl.ds(0, 96)]] + [strips.at[pl.ds(16 * s, 16)] for s in range(6)],
        [xk.at[s] for s in spans],
    )


    loaded(6)
    dmx[7] = d_merged[...]
    cd = exchange(near["y"][1], lambda t: d_merged, dmx, tsem_d.at[0], tsem_d.at[1])

    order = one_hot(token_of(along(0, 128)), token_row)
    feature = along(1, 256)
    row_a[...] = one_hot(row_a_of(along(0, 256)), feature)
    row_b[...] = one_hot(row_b_of(along(0, 128)), token_row)
    ones_t[...] = one_hot(along(0, 256) >> 6, feature >> 6)
    allowed[...] = allowed_keys(row, col)

    loaded(1, 2, 3)
    ones = ones_t[...]
    gains = gain[...]
    lane = lax.broadcasted_iota(jnp.int32, (1, 256), 1) // 64
    scales = jnp.zeros((1, 256), F32)
    for h in range(4):
        scales = jnp.where(lane == h, head_scale[:, h : h + 1], scales)
    xp = moved(order, tokens[...])
    x = xp.astype(F32)
    inverse, normed = norm_rows(x, gains)
    xhat[:OWN] = x * inverse
    nt_all[:, :OWN] = nt(row_a[...], normed).astype(BF16)
    qkv = nn(normed, w_qkv[...])
    q, k = qkv[:, :256], qkv[:, 256:512]
    q_norm = lax.rsqrt(head_sums(q * q, ones) + EPS)
    k_norm = lax.rsqrt(head_sums(k * k, ones) + EPS)
    q_unit, k_unit = q * q_norm, k * k_norm
    q_hat = (q_unit * scales).astype(BF16)
    keep[0], keep[1] = q_norm, q_unit
    keys[0, :OWN], keys[1, :OWN] = k_norm, k_unit
    kv[:OWN, :256] = k_unit.astype(BF16)
    kv[:OWN, 256:] = qkv[:, 512:].astype(BF16)
    zero = jnp.zeros((), BF16)
    for h in range(4):
        q4[128 * h : 128 * h + 128] = jnp.where(lane == h, q_hat, zero)

    loaded(4, 5, 7)
    d_group = nt(d_merged[...], w_merge[...])
    d_y = moved(order, d_skip[...]).astype(F32) + jnp.concatenate(
        [d_group[:, 256 * g : 256 * g + 256] for g in range(4)], axis=0)
    dy_b = d_y.astype(BF16)
    keep[2] = d_y
    d_attn = nt(dy_b, w_out[...]).astype(BF16)
    for h in range(4):
        da4[128 * h : 128 * h + 128] = jnp.where(lane == h, d_attn, zero)


    st[:OWN] = nt(kv[:OWN, :256], q4[...])
    dwt[:OWN] = nt(kv[:OWN, 256:], da4[...])
    for h in range(4):
        span = slice(128 * h, 128 * h + 128)
        st[:OWN, span] = jnp.exp(st[:OWN, span]) * allowed[:OWN]
    eye = one_hot(along(0, 256), feature)
    kvt[:256, :OWN] = nt(eye, kv[:OWN, :256]).astype(BF16)
    kvt[256:, :OWN] = nt(eye, kv[:OWN, 256:]).astype(BF16)

    arrived(ch, sent)
    xh = xk[...].astype(F32)
    inverse_h, normed_h = norm_rows(xh, gains)
    kv_h = nn(normed_h, w_qkv[:, 256:])
    k_h = kv_h[:, :256]
    k_norm_h = lax.rsqrt(head_sums(k_h * k_h, ones) + EPS)
    k_unit_h = k_h * k_norm_h
    keys[0, OWN:], keys[1, OWN:] = k_norm_h, k_unit_h
    kv[OWN:, :256] = k_unit_h.astype(BF16)
    kv[OWN:, 256:] = kv_h[:, 256:].astype(BF16)

    st[OWN:] = nt(kv[OWN:, :256], q4[...])
    dwt[OWN:] = nt(kv[OWN:, 256:], da4[...])
    for h in range(4):
        span = slice(128 * h, 128 * h + 128)
        e = jnp.exp(st[OWN:, span]) * allowed[OWN:]
        own = st[:OWN, span]
        r = 1.0 / (jnp.sum(own, axis=0, keepdims=True) + jnp.sum(e, axis=0, keepdims=True))
        p, p_own = e * r, own * r
        ptb[:OWN, span] = p_own.astype(BF16)
        ptb[OWN:, span] = p.astype(BF16)

        dw, dw_own = dwt[OWN:, span], dwt[:OWN, span]
        mean = jnp.sum(dw * p, axis=0, keepdims=True) + jnp.sum(dw_own * p_own, axis=0, keepdims=True)
        dst[:OWN, span] = (p_own * (dw_own - mean)).astype(BF16)
        dst[OWN:, span] = (p * (dw - mean)).astype(BF16)
    d_k = nn(dst[...], q4[...])
    ku = keys[1]
    d_kraw = (keys[0] * (d_k - ku * head_sums(ku * d_k, ones))).astype(BF16)
    d_v = nn(ptb[...], da4[...]).astype(BF16)
    nt_all[:, OWN:] = nt(row_a[...], normed_h).astype(BF16)
    normed_t = nt_all[...]
    kvt[:256, OWN:] = nt(eye, kv[OWN:, :256]).astype(BF16)
    kvt[256:, OWN:] = nt(eye, kv[OWN:, 256:]).astype(BF16)

    def diagonal(full):
        return jnp.concatenate([full[64 * h : 64 * h + 64, 128 * h : 128 * h + 128] for h in range(4)], axis=0)

    d_qhat = diagonal(nn(kvt[:256], dst[...])).T
    u = keep[1]
    g_u = d_qhat * scales
    d_q = (keep[0] * (g_u - u * head_sums(u * g_u, ones))).astype(BF16)
    attn_t = diagonal(nn(kvt[256:], ptb[...]))
    ga[:, :256] = nn(normed_t[:, :OWN], d_q).astype(BF16)
    ga[:, 256:512] = nn(normed_t, d_kraw).astype(BF16)
    ga[:, 512:768] = nn(normed_t, d_v).astype(BF16)
    ga[:, 768:] = nn(nn(row_a[...], attn_t.astype(BF16)).astype(BF16), keep[2].astype(BF16)).astype(BF16)
    mine = lambda size, index: pl.ds(pl.multiple_of(index * size, size), size)
    ca = exchange(near["core"][1], lambda t: ga.at[mine(128, t)], ra1, *sems(tsem_a, 0))

    attn = attn_t.T.astype(BF16)
    skip = (xp.astype(F32) + nn(attn, w_out[...])).astype(BF16)
    skips[...] = skip
    cb = exchange(
        near["y"][1], lambda t: skips.at[mine(32, t >> 1), mine(128, t & 1)], gx, tsem_b.at[0, :7], tsem_b.at[1, :7])

    d_normed_h = nt(d_kraw[OWN:], w_qkv[:, 256:512]) + nt(d_v[OWN:], w_qkv[:, 512:])
    hs[...] = d_normed_h.astype(BF16)
    arrived(ca, sent)
    sa2[...] = (ga[mine(128, core)].astype(F32) + ra1[0].astype(F32)).astype(BF16)
    ca = exchange(near["x"][1], lambda t: sa2.at[mine(32, t)], ra2, *sems(tsem_a, 1))
    ch = halo(1, reverse, [hs.at[s] for s in spans], [hr.at[s] for s in spans])

    d_normed = (nt(d_q, w_qkv[:, :256]) + nt(d_kraw[:OWN], w_qkv[:, 256:512])) + nt(d_v[:OWN], w_qkv[:, 512:])
    gain_row = jnp.sum(xhat[:OWN] * d_normed, axis=0, keepdims=True) + jnp.sum(
        xh * inverse_h * d_normed_h, axis=0, keepdims=True)
    scale_row = jnp.sum(u * d_qhat, axis=0, keepdims=True)
    for i, r in enumerate((gain_row[:, :128], gain_row[:, 128:], scale_row[:, :128], scale_row[:, 128:])):
        g1[core, i : i + 1] = r
    g1[core, 4:8] = jnp.zeros((4, 128), F32)
    cg = spread(core, near["core"][1], g1, *sems(tsem_g, 0))

    unorder = one_hot(place_of(along(0, 128)), token_row)
    o_skip[...] = moved(unorder, skip)
    group = jnp.concatenate([skip[32 * g : 32 * g + 32] for g in range(4)], axis=1)
    o_merged[...] = nn(group, w_merge[...]).astype(BF16)
    saves[0].start()
    saves[1].start()
    arrived(cg, sent)
    g2[x_at] = g1[0] + g1[1]
    cg = spread(x_at, near["x"][1], g2, *sems(tsem_g, 1))

    gx[7] = skips[mine(32, y_at >> 1), mine(128, y_at & 1)]
    arrived(cd, sent)
    arrived(cb, sent)
    factor = nt(row_b[...], gx[...].reshape(256, 128)).astype(BF16)
    gb[...] = nn(factor, dmx[...].reshape(256, 512)).astype(BF16)
    cb = exchange(near["core"][1], lambda t: gb.at[mine(64, t)], rb1, tsem_b.at[0, 7:8], tsem_b.at[1, 7:8])

    arrived(ca, sent)
    total = sa2[mine(32, x_at)].astype(F32)
    for p in range(3):
        total = total + ra2[p].astype(F32)
    total = jnp.concatenate(
        [jnp.concatenate([total[:, 192 * c : 192 * c + 192], total[:, 768 + 64 * c : 832 + 64 * c]], axis=1)
         for c in range(4)], axis=0)
    sa3[...] = moved(one_hot(slab_of(along(0, 128)), token_row), total.astype(BF16)).reshape(8, 16, 256)
    ca = exchange(near["y"][1], lambda t: sa3.at[t], ra3, *sems(tsem_a, 2))
    arrived(cg, sent)
    g3[y_at] = (g2[0] + g2[1]) + (g2[2] + g2[3])
    cg = spread(y_at, near["y"][1], g3, *sems(tsem_g, 2))
    arrived(cb, sent)
    sb2[...] = (gb[mine(64, core)].astype(F32) + rb1[0].astype(F32)).astype(BF16)
    cb = exchange(near["x"][1], lambda t: sb2.at[mine(16, t)], rb2, tsem_b.at[0, 8:11], tsem_b.at[1, 8:11])

    arrived(ch, sent)
    d_normed = d_normed + nn(one_hot(token_of(along(0, 128)), sent_token(along(1, HALO))), hr[...])
    scaled = gains * d_normed
    x = xp.astype(F32)
    g_x = inverse * scaled - x * (inverse * inverse * inverse) * jnp.mean(x * scaled, axis=-1, keepdims=True)
    o_tokens[...] = moved(unorder, (keep[2] + g_x).astype(BF16))
    saves[2].start()

    arrived(cb, sent)
    total = sb2[mine(16, x_at)].astype(F32)
    for p in range(3):
        total = total + rb2[p].astype(F32)
    sb4[...] = total
    cb = exchange(
        near["z"][1], lambda t: sb4.at[mine(8, t & 1), mine(128, t >> 1)], rb4, tsem_b.at[0, 11:], tsem_b.at[1, 11:])

    arrived(ca, sent)
    total = sa3[y_at].astype(F32)
    for p in range(7):
        total = total + ra3[p].astype(F32)
    sa4[...] = total.reshape(2, 8, 256)
    ca = exchange(near["z"][1], lambda t: sa4.at[t >> 2], ra4, *sems(tsem_a, 3))
    arrived(cg, sent)
    g4[z_at] = ((g3[0] + g3[1]) + (g3[2] + g3[3])) + ((g3[4] + g3[5]) + (g3[6] + g3[7]))
    cg = spread(z_at, near["z"][1], g4, *sems(tsem_g, 3))

    drain(sent)
    for c in ca + cb + cg:
        c.wait_send()
    last = []
    arrived(cb, last)
    total = sb4[mine(8, z_at & 1), mine(128, z_at >> 1)]
    for p in range(7):
        total = total + rb4[p]
    o_merge[...] = total
    saves[5].start()
    arrived(ca, last)
    total = sa4[z_at >> 2]
    for p in range(7):
        total = total + ra4[p]
    part = z_at & 3
    piece = jnp.zeros((2, 256), F32)
    for i in range(4):
        piece = piece + jnp.where(part == i, total[2 * i : 2 * i + 2], 0.0)
    o_qkv[...] = piece[:, :192]
    o_out[...] = piece[:, 192:]
    saves[3].start()
    saves[4].start()
    arrived(cg, last)
    total = ((g4[0] + g4[1]) + (g4[2] + g4[3])) + ((g4[4] + g4[5]) + (g4[6] + g4[7]))
    o_gain[...] = total[0:2]
    halves = lax.broadcasted_iota(jnp.int32, (1, 128), 1)
    out = jnp.zeros((1, 128), F32)
    for h in range(4):
        r = total[2 + h // 2 : 3 + h // 2]
        out = jnp.where(halves == h, jnp.sum(jnp.where(halves // 64 == h % 2, r, 0.0), axis=1, keepdims=True), out)
    o_scale[...] = out[:, :4]
    saves[6].start()
    saves[7].start()
    wait_copies(saves)


def hand_over(*refs):
    sources, targets, held, sem = refs[:8], refs[8:16], refs[16:24], refs[24]
    loads = start_copies([pltpu.make_async_copy(s, h, sem.at[0, i]) for i, (s, h) in enumerate(zip(sources, held))])
    saves = [pltpu.make_async_copy(h, t, sem.at[1, i]) for i, (h, t) in enumerate(zip(held, targets))]
    for load, save in zip(loads, saves):
        load.wait()
        save.start()
    wait_copies(saves)


def on_device(tokens, gain, w_qkv, head_scale, w_out, w_merge, d_merged, d_skip):
    V = pltpu.VMEM
    S = jax.ShapeDtypeStruct
    DMA = pltpu.SemaphoreType.DMA
    operands = (
        tokens.reshape(128, 256), gain.reshape(1, 256), w_qkv, head_scale.reshape(1, 4), w_out, w_merge,
        d_merged.reshape(32, 512), d_skip.reshape(128, 256),
    )
    results = (
        S((128, 256), BF16), S((32, 512), BF16), S((128, 256), BF16),
        S((2, 192), F32), S((2, 64), F32), S((8, 128), F32), S((2, 128), F32), S((1, 4), F32),
    )
    far = pl.BlockSpec(memory_space=pltpu.MemorySpace.HBM)
    out = pl.pallas_call(
        body,
        out_shape=results,
        in_specs=[far] * 8,
        out_specs=(far,) * 8,
        scratch_shapes=[V(a.shape, a.dtype) for a in operands + results] + [
            DMA((8,)), DMA((8,)),
            V((HALO, 256), BF16), V((96, 256), BF16), V((256, 256), BF16), V((128, 128), BF16), V((256, 256), BF16),
            V((NK, 512), BF16), V((512, NK), BF16),
            V((NK, 512), F32), V((NK, 512), F32), V((NK, 512), BF16), V((NK, 512), BF16),
            V((512, 256), BF16), V((512, 256), BF16), V((3, 128, 256), F32), V((2, NK, 256), F32), V((OWN, 256), F32),
            V((256, NK), BF16), V((HALO, 256), BF16), V((HALO, 256), BF16), V((NK, 128), F32),
            V((256, 1024), BF16), V((1, 128, 1024), BF16),
            V((128, 1024), BF16), V((3, 32, 1024), BF16),
            V((8, 16, 256), BF16), V((7, 16, 256), BF16),
            V((2, 8, 256), F32), V((7, 8, 256), F32),
            V((128, 256), BF16), V((8, 32, 128), BF16), V((8, 32, 512), BF16),
            V((128, 512), BF16), V((1, 64, 512), BF16),
            V((64, 512), BF16), V((3, 16, 512), BF16),
            V((16, 512), F32), V((7, 8, 128), F32),
            V((2, 8, 128), F32), V((4, 8, 128), F32), V((8, 8, 128), F32), V((8, 8, 128), F32),
            DMA((2, 28)), DMA((2, 18)), DMA((2, 7)), DMA((2, 28)), DMA((2, 16)),
        ],
        compiler_params=pltpu.CompilerParams(collective_id=0, has_side_effects=True, vmem_limit_bytes=VMEM_LIMIT),
    )(*operands)
    out = pl.pallas_call(
        hand_over,
        out_shape=results,
        in_specs=[far] * 8,
        out_specs=(far,) * 8,
        scratch_shapes=[V(a.shape, a.dtype) for a in results] + [DMA((2, 8))],
        compiler_params=pltpu.CompilerParams(vmem_limit_bytes=VMEM_LIMIT),
    )(*out)
    skip, merged, grad, qkv, o, m, g, s = out
    return (skip.reshape(4, 32, 256), merged.reshape(2, 16, 512), grad.reshape(4, 32, 256), qkv, o, m, g.reshape(256), s.reshape(4))


def solution(mesh):
    return jax.shard_map(
        on_device,
        mesh=mesh,
        in_specs=(
            P("row", "col", None),
            P(),
            P(),
            P(),
            P(),
            P(),
            P("row", "col", None),
            P("row", "col", None),
        ),
        out_specs=(
            P("row", "col", None),
            P("row", "col", None),
            P("row", "col", None),
            P("row", "col"),
            P("row", "col"),
            P("row", "col"),
            P(),
            P(),
        ),
        check_vma=False,
    )
```
